256 devices in a mesh: pipe: 8 (over z_hi, core), dp: 32 (over z_lo, y, x).
Axes of the slice: x: 4, y: 4, z: 8 (z_hi: 4, z_lo: 2; z = z_hi * 2 + z_lo), core: 2. Of those that a mesh axis runs over, the one named last changes fastest.
Arguments:
- item_ids: int32 [4, 1056], P(None, 'dp'), may hold values from 0 to 127
- plan_order: int32 [4], replicated, may hold values from 0 to 3, each once
- candidates: bfloat16 [128, 3072], replicated, may hold values from -6 to 6
- adapters_in: bfloat16 [8, 2, 3072, 256], P('pipe'), may hold values from -0.109375 to 0.109375
- adapters_out: bfloat16 [8, 2, 256, 3072], P('pipe'), may hold values from -0.1875 to 0.1875
Outputs:
- grad_in: float32 [8, 2, 3072, 256], P('pipe', None, 'dp')
- grad_out: float32 [8, 2, 256, 3072], P('pipe', None, None, 'dp')
The draws below stay inside these ranges and needn't reach their ends.
Inputs may be any that keep to these rules, and one draw needn't show every extreme that they name: `plan_order`: a permutation of the micro-batches.
All inputs are finite; a program needn't handle non-finite values.
Results may differ from the reference program's by a relative error of at most 0.025.
Values may be sent and summed in bfloat16 or wider, within the bound.
A program may use at most 128 MiB of HBM per device.

```python
import math
import jax
import jax.numpy as jnp
from jax import lax

D = 3072
H = 256
EVENTS = 32
MICRO = 4
CAND = 128
N_PIPE = 8
N_DP = 32


def touch_ends(array, own_key, least, largest):
    extent = array.shape
    place = [jax.random.randint(jax.random.fold_in(own_key, axis), (), 0, extent[axis]) for axis in range(len(extent))]
    array = array.at[tuple(place)].set(least)
    longest = extent.index(max(extent))
    place[longest] = (place[longest] + 1) % extent[longest]
    return array.at[tuple(place)].set(largest)


def shard_levels(key, shape, split, least, top_value):
    loudness, own = 1.0, jax.random.fold_in(key, 6)
    for axis_at, parts in split:
        heights = jnp.exp(jax.random.uniform(jax.random.fold_in(own, axis_at), (parts,), jnp.float32, least / len(split), top_value / len(split)))
        loudness = loudness * jnp.repeat(heights, shape[axis_at] // parts).reshape([-1 if axis == axis_at else 1 for axis in range(len(shape))])
    return loudness


def bell_draw(stream_key, shape, spread, limit, split=(), dtype=jnp.bfloat16):
    level = shard_levels(stream_key, shape, split, -0.22, 0.18) if split else 1.0
    result = jax.random.normal(stream_key, shape, jnp.float32) * spread * level
    return jnp.minimum(jnp.maximum(result, -limit), limit).astype(dtype)


def setup_inputs(seed: int = 0) -> dict:
    streams_of = jax.random.split(jax.random.key(seed), 6)
    return {
        "item_ids": touch_ends(jax.random.randint(streams_of[0], (MICRO, (EVENTS + 1) * N_DP), 0, CAND), jax.random.fold_in(streams_of[0], 1), 0, CAND - 1).astype(jnp.int32),
        "plan_order": jax.random.permutation(streams_of[1], MICRO).astype(jnp.int32),
        "candidates": bell_draw(streams_of[2], (CAND, D), 1.0, 6.0),
        "adapters_in": bell_draw(streams_of[3], (N_PIPE, 2, D, H), D ** -0.5, 0.109375, ((0, 8),)),
        "adapters_out": bell_draw(streams_of[4], (N_PIPE, 2, H, D), (4 * H) ** -0.5, 0.1875, ((0, 8),)),
    }


def advance(inputs, w_first, w_second):
    pre_act = jnp.dot(inputs, w_first, preferred_element_type=jnp.float32)
    activated = jax.nn.silu(pre_act).astype(jnp.bfloat16)
    branch = jnp.dot(activated, w_second, preferred_element_type=jnp.float32)
    return ((inputs.astype(jnp.float32) + branch).astype(jnp.bfloat16), pre_act)

def retreat(inputs, pre_act, w_first, w_second, grad_y):
    logistic = jax.nn.sigmoid(pre_act)
    slope = logistic * (1.0 + pre_act * (1.0 - logistic))
    grad_act = jnp.dot(grad_y, w_second.T, preferred_element_type=jnp.float32)
    grad_pre = (grad_act * slope).astype(jnp.bfloat16)
    grad_x = (grad_y.astype(jnp.float32) + jnp.dot(grad_pre, w_first.T, preferred_element_type=jnp.float32)).astype(jnp.bfloat16)
    activated = jax.nn.silu(pre_act).astype(jnp.bfloat16)
    term_in = jnp.dot(inputs.T, grad_pre, preferred_element_type=jnp.float32)
    term_out = jnp.dot(activated.T, grad_y, preferred_element_type=jnp.float32)
    return (grad_x, term_in, term_out)

def weights_of(layer_index):
    if layer_index < N_PIPE:
        return (layer_index, 0)
    return (2 * N_PIPE - 1 - layer_index, 1)

def run_path(layer_path, first_inputs, seed_grad, adapters_in, adapters_out):
    inputs = first_inputs
    stash = []
    for layer_index in layer_path:
        section_index, block_index = weights_of(layer_index)
        outputs, pre_act = advance(inputs, adapters_in[section_index, block_index], adapters_out[section_index, block_index])
        stash.append((inputs, pre_act))
        inputs = outputs
    sum_in = jnp.zeros(adapters_in.shape, jnp.float32)
    sum_out = jnp.zeros(adapters_out.shape, jnp.float32)
    grad_y = seed_grad
    for position in range(len(layer_path) - 1, -1, -1):
        section_index, block_index = weights_of(layer_path[position])
        saved_in, saved_pre = stash[position]
        grad_y, term_in, term_out = retreat(saved_in, saved_pre, adapters_in[section_index, block_index], adapters_out[section_index, block_index], grad_y)
        sum_in = sum_in.at[section_index, block_index].add(term_in)
        sum_out = sum_out.at[section_index, block_index].add(term_out)
    return (sum_in, sum_out)

def reference(item_ids, plan_order, candidates, adapters_in, adapters_out):
    segments = item_ids.reshape(MICRO, N_DP, EVENTS + 1)
    scale = 1.0 / math.sqrt(MICRO * N_DP * EVENTS)
    front_path = list(range(2 * N_PIPE))
    back_path = list(range(N_PIPE, 2 * N_PIPE)) + list(range(N_PIPE))
    grad_in = jnp.zeros(adapters_in.shape, jnp.float32)
    grad_out = jnp.zeros(adapters_out.shape, jnp.float32)
    for batch_index in range(MICRO):
        events = segments[batch_index, :, :EVENTS].reshape(-1)
        targets = segments[batch_index, :, 1:].reshape(-1)
        embedded = jnp.take(candidates, events, axis=0)
        seed_grad = (jnp.take(candidates, targets, axis=0).astype(jnp.float32) * scale).astype(jnp.bfloat16)
        from_front = plan_order[batch_index] < MICRO // 2
        sum_in, sum_out = lax.cond(from_front, lambda: run_path(front_path, embedded, seed_grad, adapters_in, adapters_out), lambda: run_path(back_path, embedded, seed_grad, adapters_in, adapters_out))
        grad_in = grad_in + sum_in
        grad_out = grad_out + sum_out
    return (grad_in, grad_out)
```

```python
import functools
import math

import jax
import jax.numpy as jnp
from jax import lax
from jax.experimental import pallas as pl
from jax.experimental.pallas import tpu as pltpu
from jax.sharding import PartitionSpec as P

MESH = pl.DeviceIdType.MESH
F32 = jnp.float32
BF16 = jnp.bfloat16


def mm(a, b):
    return jnp.dot(a, b, preferred_element_type=F32)


def mm_t(a, b):
    return lax.dot_general(a, b, (((1,), (1,)), ((), ())), preferred_element_type=F32)


def t_mm(a, b):
    return lax.dot_general(a, b, (((0,), (0,)), ((), ())), preferred_element_type=F32)


def fold(wide):
    half = wide.shape[1] // 2
    return jnp.concatenate([wide[:, :half], wide[:, half:]], axis=0)


def twice(rows):
    return jnp.concatenate([rows, rows], axis=0).astype(BF16)


def kernel(
    n_pipe,
    n_dp,
    scale,
    ids_ref,
    cand_ref,
    win_ref,
    wout_ref,
    gin_ref,
    gout_ref,
    w_in,
    w_out,
    got,
    give,
    pres,
    ids_all,
    sbuf,
    rbuf,
    w_sem,
    give_sem,
    got_sem,
    ids_send,
    ids_recv,
    x_send,
    x_recv,
):
    p = lax.axis_index("pipe")
    d = lax.axis_index("dp")
    half_dp = n_dp // 2
    path = d // half_dp
    block = d % half_dp
    c1 = path
    c2 = 1 - path
    last = n_pipe - 1
    q = p + path * (last - 2 * p)
    up = p + 1 - 2 * path
    down = p - 1 + 2 * path
    half = w_in.shape[1] // 2
    share = 2 * half // n_dp

    def load(c):
        return (
            pltpu.make_async_copy(win_ref.at[0, c], w_in.at[c], w_sem.at[c, 0]),
            pltpu.make_async_copy(wout_ref.at[0, c], w_out.at[c], w_sem.at[c, 1]),
        )

    for c in (c1, c2):
        for copy in load(c):
            copy.start()

    barrier = pltpu.get_barrier_semaphore()
    for step in (1, n_pipe - 1):
        pl.semaphore_signal(
            barrier, inc=1, device_id={"pipe": lax.rem(p + step, n_pipe)}, device_id_type=MESH
        )

    def greet(k, carry):
        pl.semaphore_signal(
            barrier, inc=1, device_id={"dp": lax.rem(d + k, n_dp)}, device_id_type=MESH
        )
        return carry

    lax.fori_loop(1, n_dp, greet, 0)
    pl.semaphore_wait(barrier, n_dp + 1)

    def hop(slot, to):
        return pltpu.make_async_remote_copy(
            src_ref=give.at[slot],
            dst_ref=got.at[slot],
            send_sem=give_sem.at[slot],
            recv_sem=got_sem.at[slot],
            device_id={"pipe": to},
            device_id_type=MESH,
        )

    def spread_ids():
        ids_all[d] = ids_ref[...]

        def send(k, carry):
            pltpu.make_async_remote_copy(
                src_ref=ids_ref,
                dst_ref=ids_all.at[d],
                send_sem=ids_send,
                recv_sem=ids_recv,
                device_id={"dp": lax.rem(d + k, n_dp)},
                device_id_type=MESH,
            ).start()
            return carry

        lax.fori_loop(1, n_dp, send, 0)

    def spread(c, kind, small, big):
        hidden = small.shape[1] // 2
        top = jnp.concatenate([small[:, :hidden], small[:, hidden:]], axis=0).astype(BF16)
        wide = jnp.concatenate([big, big[:, :128]], axis=1)
        for j in range(half_dp):
            sbuf[c, kind, j, 0:16, :] = top
            sbuf[c, kind, j, 16:32, :] = wide[:, share * j : share * j + 128].astype(BF16)
        rbuf[c, kind, d] = sbuf[c, kind, block]

        def send(k, carry):
            peer = lax.rem(d + k, n_dp)
            pltpu.make_async_remote_copy(
                src_ref=sbuf.at[c, kind, lax.rem(peer, half_dp)],
                dst_ref=rbuf.at[c, kind, d],
                send_sem=x_send.at[c, kind],
                recv_sem=x_recv.at[c, kind],
                device_id={"dp": peer},
                device_id_type=MESH,
            ).start()
            return carry

        lax.fori_loop(1, n_dp, send, 0)

    def many(ref, sem):
        return pltpu.make_async_copy(ref, ref, sem)

    def forward(c, slot):
        x2 = got[slot]
        pre = mm(x2, w_in[c, :half, :])[:8] + mm(x2, w_in[c, half:, :])[8:]
        act = pre / (1.0 + jnp.exp(-pre))
        pres[c] = pre
        branch = mm(twice(act), w_out[c])[:8]
        y2 = (x2.astype(F32) + fold(branch)).astype(BF16)
        give[slot] = y2
        return x2, act

    def backward(c, slot, want):
        g2 = got[slot]
        grad_act = mm_t(g2, w_out[c, :, :half])[:8] + mm_t(g2, w_out[c, :, half:])[8:]
        pre = pres[c]
        logistic = 1.0 / (1.0 + jnp.exp(-pre))
        grad_pre = grad_act * (logistic * (1.0 + pre * (1.0 - logistic)))

        @pl.when(want)
        def _():
            term = mm_t(twice(grad_pre), w_in[c])[:8]
            give[slot] = (g2.astype(F32) + fold(term)).astype(BF16)

        return g2, grad_pre

    def finish(c):
        for kind in (0, 1):
            many(rbuf.at[c, kind, pl.ds(0, n_dp - 1)], x_recv.at[c, kind]).wait()

        def unpack(kind):
            rows = rbuf[c, kind].astype(F32)
            flat = lambda part: part.reshape(n_dp * 8, 128)
            small = jnp.concatenate([flat(rows[:, 0:8]), flat(rows[:, 8:16])], axis=1)
            big = jnp.where(path == 0, flat(rows[:, 16:24]), flat(rows[:, 24:32]))
            return small.astype(BF16), big.astype(BF16)

        act, x = unpack(0)
        grad_pre, grad_y = unpack(1)
        gin_ref[0, c] = t_mm(x, grad_pre)[:share]
        gout_ref[0, c] = t_mm(act, grad_y)[:, :share]

    @pl.when(q == last)
    def _():
        spread_ids()

    @pl.when(q == 0)
    def _():
        start = pl.multiple_of(16 * (block // 2), 16)
        rows = cand_ref[pl.ds(start, 16), :].astype(F32)
        mine = jnp.where(block % 2 == 0, rows[:8], rows[8:])
        got[0] = fold(mine).astype(BF16)

    @pl.when(q > 0)
    def _():
        hop(0, down).wait_recv()

    for copy in load(c1):
        copy.wait()
    x2, act = forward(c1, 0)

    @pl.when(q < last)
    def _():
        hop(0, up).start()

    @pl.when(q == last)
    def _():
        got[1] = give[0]

    @pl.when(q == 0)
    def _():
        spread_ids()

    spread(c1, 0, act, x2.astype(F32))

    @pl.when((q == 0) | (q == last))
    def _():
        many(ids_all.at[pl.ds(0, n_dp - 1)], ids_recv).wait()

    @pl.when(q == 0)
    def _():
        own = lax.broadcasted_iota(jnp.int32, (16, 128), 0) + 8 * block
        every = lax.broadcasted_iota(jnp.int32, (128, 128), 0)

        def count(group, total):
            left, right = [], []
            for k in range(8):
                tile = ids_all[group * 8 + k]
                events = jnp.where(path == 0, tile[0:1, :], tile[1:2, :])
                left.append(jnp.where(own == events, 1.0, 0.0).astype(BF16))
                right.append(jnp.where(every == tile[2:3, :], 1.0, 0.0).astype(BF16))
            return total + mm_t(jnp.concatenate(left, axis=1), jnp.concatenate(right, axis=1))

        counts = lax.fori_loop(0, n_dp // 8, count, jnp.zeros((16, 128), F32))[:8]
        sixteens = jnp.floor(counts * 0.0625)
        parts = jnp.concatenate([sixteens, counts - 16.0 * sixteens], axis=0).astype(BF16)
        sums = mm(parts, cand_ref[...])
        got[2] = fold((16.0 * sums[:8] + sums[8:]) * scale).astype(BF16)

    @pl.when(q < last)
    def _():
        hop(1, up).wait_recv()

    for copy in load(c2):
        copy.wait()
    x2, act = forward(c2, 1)

    @pl.when(q > 0)
    def _():
        hop(1, down).start()

    spread(c2, 0, act, x2.astype(F32))

    @pl.when(q > 0)
    def _():
        hop(2, down).wait_recv()

    g2, grad_pre = backward(c2, 2, q >= 0)

    @pl.when(q < last)
    def _():
        hop(2, up).start()

    @pl.when(q == last)
    def _():
        got[3] = give[2]

    spread(c2, 1, grad_pre, g2.astype(F32))

    @pl.when(q <= 2)
    def _():
        finish(c2)

    @pl.when(q < last)
    def _():
        hop(3, up).wait_recv()

    g2, grad_pre = backward(c1, 3, q > 0)

    @pl.when(q > 0)
    def _():
        hop(3, down).start()

    spread(c1, 1, grad_pre, g2.astype(F32))
    finish(c1)

    @pl.when(q > 2)
    def _():
        finish(c2)

    @pl.when(q < last)
    def _():
        hop(0, up).wait_send()
        hop(2, up).wait_send()

    @pl.when(q > 0)
    def _():
        hop(1, down).wait_send()
        hop(3, down).wait_send()

    @pl.when((q == 0) | (q == last))
    def _():
        many(ids_all.at[pl.ds(0, n_dp - 1)], ids_send).wait()

    for c in (0, 1):
        for kind in (0, 1):
            many(rbuf.at[c, kind, pl.ds(0, n_dp - 1)], x_send.at[c, kind]).wait()


def local(n_pipe, n_dp, item_ids, plan_order, candidates, adapters_in, adapters_out):
    batches, width = item_ids.shape
    events = width - 1
    _, _, features, hidden = adapters_in.shape
    share = features // n_dp
    scale = 1.0 / math.sqrt(batches * n_dp * events)
    event = item_ids[:, :events].reshape(1, batches * events)
    target = item_ids[:, 1:].reshape(1, batches * events)
    front = jnp.repeat(plan_order < batches // 2, events).reshape(1, batches * events)
    ids = jnp.concatenate(
        [
            jnp.where(front, event, -1),
            jnp.where(front, -1, event),
            target,
            jnp.zeros((5, batches * events), jnp.int32),
        ],
        axis=0,
    )
    vmem = pl.BlockSpec(memory_space=pltpu.VMEM)
    anywhere = pl.BlockSpec(memory_space=pl.ANY)
    return pl.pallas_call(
        functools.partial(kernel, n_pipe, n_dp, scale),
        out_shape=(
            jax.ShapeDtypeStruct((1, 2, share, hidden), F32),
            jax.ShapeDtypeStruct((1, 2, hidden, share), F32),
        ),
        in_specs=[vmem, vmem, anywhere, anywhere],
        out_specs=(vmem, vmem),
        scratch_shapes=[
            pltpu.VMEM((2, features, hidden), BF16),
            pltpu.VMEM((2, hidden, features), BF16),
            pltpu.VMEM((4, 16, features // 2), BF16),
            pltpu.VMEM((4, 16, features // 2), BF16),
            pltpu.VMEM((2, 8, hidden), F32),
            pltpu.VMEM((n_dp, 8, 128), jnp.int32),
            pltpu.VMEM((2, 2, n_dp // 2, 32, 128), BF16),
            pltpu.VMEM((2, 2, n_dp, 32, 128), BF16),
            pltpu.SemaphoreType.DMA((2, 2)),
            pltpu.SemaphoreType.DMA((4,)),
            pltpu.SemaphoreType.DMA((4,)),
            pltpu.SemaphoreType.DMA,
            pltpu.SemaphoreType.DMA,
            pltpu.SemaphoreType.DMA((2, 2)),
            pltpu.SemaphoreType.DMA((2, 2)),
        ],
        compiler_params=pltpu.CompilerParams(
            collective_id=0, has_side_effects=True, vmem_limit_bytes=40 * 1024 * 1024
        ),
    )(ids, candidates, adapters_in, adapters_out)


def solution(mesh):
    in_specs = (P(None, "dp"), P(), P(), P("pipe", None, None, None), P("pipe", None, None, None))
    out_specs = (P("pipe", None, "dp", None), P("pipe", None, None, "dp"))
    return jax.shard_map(
        functools.partial(local, mesh.shape["pipe"], mesh.shape["dp"]),
        mesh=mesh,
        in_specs=in_specs,
        out_specs=out_specs,
        check_vma=False,
    )
```

```python
import functools
import math

import jax
import jax.numpy as jnp
from jax import lax
from jax.experimental import pallas as pl
from jax.experimental.pallas import tpu as pltpu
from jax.sharding import PartitionSpec as P

MESH = pl.DeviceIdType.MESH
F32 = jnp.float32
BF16 = jnp.bfloat16
PIECES = 3


def mm(a, b):
    return jnp.dot(a, b, preferred_element_type=F32)


def mm_t(a, b):
    return lax.dot_general(a, b, (((1,), (1,)), ((), ())), preferred_element_type=F32)


def t_mm(a, b):
    return lax.dot_general(a, b, (((0,), (0,)), ((), ())), preferred_element_type=F32)


def fold(wide):
    half = wide.shape[1] // 2
    return jnp.concatenate([wide[:, :half], wide[:, half:]], axis=0)


def twice(rows):
    return jnp.concatenate([rows, rows], axis=0).astype(BF16)


def kernel(
    n_pipe,
    n_dp,
    scale,
    ids_hbm,
    cand_hbm,
    win_ref,
    wout_ref,
    gin_ref,
    gout_ref,
    w_in,
    w_out,
    t_in,
    t_out,
    m_fwd,
    m_bwd,
    ids_ref,
    cand_ref,
    first_rows,
    ids_own,
    ids_all,
    got,
    mid,
    give,
    small,
    slopes,
    mail_big,
    mail_small,
    sbuf,
    rbuf,
    x_turned,
    act_rows,
    w_sem,
    cand_sem,
    share_send,
    share_recv,
    give_sem,
    got_sem,
    mail_send,
    mail_recv,
    back_send,
    back_recv,
    ids_send,
    ids_recv,
    x_send,
    x_recv,
):
    p = lax.axis_index("pipe")
    d = lax.axis_index("dp")
    half_dp = n_dp // 2
    path = d // half_dp
    block = d % half_dp
    c1 = path
    c2 = 1 - path
    chips = n_pipe // 2
    chip = p // 2
    core = p % 2
    relay = core == path
    other = p + 1 - 2 * core
    last = chips - 1
    k = chip + path * (last - 2 * chip)
    up = p + 2 - 4 * path
    down = p - 2 + 4 * path
    edge = (p == 0) | (p == n_pipe - 1)
    up_first = other + 2 - 4 * path
    half = w_in.shape[1] // 2
    piece = half // PIECES
    pieces = range(PIECES)
    pairs = ((c1, 2 + c1), (2 + c2, c2))
    share = 2 * half // n_dp
    cs = (c1, c2, c2, c1)

    def load(c):
        return (
            pltpu.make_async_copy(win_ref.at[0, c], w_in.at[c], w_sem.at[c, 0]),
            pltpu.make_async_copy(wout_ref.at[0, c], w_out.at[c], w_sem.at[c, 1]),
        )

    def lend(c):
        return [
            pltpu.make_async_remote_copy(
                src_ref=src.at[0, c],
                dst_ref=dst.at[2 + c],
                send_sem=share_send.at[c, n],
                recv_sem=share_recv.at[c, n],
                device_id={"pipe": other},
                device_id_type=MESH,
            )
            for n, (src, dst) in enumerate(((win_ref, w_in), (wout_ref, w_out)))
        ]

    start = pl.multiple_of(16 * (block // 2), 16)
    own_rows = pltpu.make_async_copy(cand_hbm.at[pl.ds(start, 16)], first_rows, cand_sem.at[0])
    all_rows = pltpu.make_async_copy(cand_hbm, cand_ref, cand_sem.at[1])

    id_copy = pltpu.make_async_copy(ids_hbm, ids_ref, cand_sem.at[2])

    @pl.when(relay & (k == 0))
    def _():
        own_rows.start()

    @pl.when(relay | (k == 0))
    def _():
        for copy in load(c1):
            copy.start()

    @pl.when(edge)
    def _():
        id_copy.start()

    @pl.when(relay)
    def _():
        for copy in load(c2):
            copy.start()

        @pl.when(k == 0)
        def _():
            all_rows.start()

    barrier = pltpu.get_barrier_semaphore()
    for to in (other, lax.rem(p + 2, n_pipe), lax.rem(p + n_pipe - 2, n_pipe)):
        pl.semaphore_signal(barrier, inc=1, device_id={"pipe": to}, device_id_type=MESH)

    def greet(n, carry):
        pl.semaphore_signal(
            barrier, inc=1, device_id={"dp": lax.rem(d + n, n_dp)}, device_id_type=MESH
        )
        return carry

    lax.fori_loop(1, n_dp, greet, 0)

    def far_first(n):
        side = d // 16, (d // 4) % 4, d % 4

        def away(t):
            return (2 + 3 * (t * (t + 1) // 2)) % 4

        plane = (side[0] + 1 - n % 2) % 2
        column = (side[1] + away(n // 8)) % 4
        return 16 * plane + 4 * column + (side[2] + away((n // 2) % 4)) % 4

    def piece_at(j):
        return pl.ds(j * piece, piece)

    def hop(ph, j, to):
        return pltpu.make_async_remote_copy(
            src_ref=give.at[ph, :, piece_at(j)],
            dst_ref=got.at[ph, :, piece_at(j)],
            send_sem=give_sem.at[ph, j],
            recv_sem=got_sem.at[ph, j],
            device_id={"pipe": to},
            device_id_type=MESH,
        )

    def back():
        return pltpu.make_async_remote_copy(
            src_ref=slopes.at[c1],
            dst_ref=slopes.at[2 + c1],
            send_sem=back_send,
            recv_sem=back_recv,
            device_id={"pipe": other},
            device_id_type=MESH,
        )

    def mail(ph):
        big = mid if ph in (0, 2) else got
        return [
            pltpu.make_async_remote_copy(
                src_ref=src,
                dst_ref=dst,
                send_sem=mail_send.at[ph, n],
                recv_sem=mail_recv.at[ph, n],
                device_id={"pipe": other},
                device_id_type=MESH,
            )
            for n, (src, dst) in enumerate(
                (
                    (big.at[ph], mail_big.at[ph]),
                    (small.at[ph, 1 if ph in (0, 2) else 0], mail_small.at[ph]),
                )
            )
        ]

    def spread_ids():
        id_copy.wait()
        lane = lax.broadcasted_iota(jnp.int32, (1, 128), 1)
        front = back = target = jnp.full((1, 128), -1, jnp.int32)
        ids_own[...] = jnp.full((8, 128), -1, jnp.int32)
        ids_own[0:5, 0:33] = ids_ref[...]
        plan = ids_own[4:5, :]
        for m in range(4):
            row = ids_own[m : m + 1, :]
            here = lane // 32 == m
            event = pltpu.roll(row, 32 * m, 1) if m else row
            is_front = plan[:, m : m + 1] < 2
            front = jnp.where(here & is_front, event, front)
            back = jnp.where(here & jnp.logical_not(is_front), event, back)
            target = jnp.where(here, pltpu.roll(row, (32 * m + 127) % 128, 1), target)
        ids_own[0:1, :] = front
        ids_own[1:2, :] = back
        ids_own[2:3, :] = target
        ids_all[d] = ids_own[...]

        def send(n, carry):
            pltpu.make_async_remote_copy(
                src_ref=ids_own,
                dst_ref=ids_all.at[d],
                send_sem=ids_send,
                recv_sem=ids_recv,
                device_id={"dp": lax.rem(d + n, n_dp)},
                device_id_type=MESH,
            ).start()
            return carry

        lax.fori_loop(1, n_dp, send, 0)

    def spread(ph, narrow, broad):
        c, kind = cs[ph], ph // 2
        narrow, broad = narrow[...], broad[...].astype(F32)
        hidden = narrow.shape[1] // 2
        top = jnp.concatenate([narrow[:, :hidden], narrow[:, hidden:]], axis=0).astype(BF16)
        wide = jnp.concatenate([broad, broad[:, :128]], axis=1)
        for j in range(half_dp):
            sbuf[c, kind, j, 0:16, :] = top
            sbuf[c, kind, j, 16:32, :] = wide[:, share * j : share * j + 128].astype(BF16)
        rbuf[c, kind, d] = sbuf[c, kind, block]

        def send(n, carry):
            peer = far_first(n)
            pltpu.make_async_remote_copy(
                src_ref=sbuf.at[c, kind, lax.rem(peer, half_dp)],
                dst_ref=rbuf.at[c, kind, d],
                send_sem=x_send.at[c, kind],
                recv_sem=x_recv.at[c, kind],
                device_id={"dp": peer},
                device_id_type=MESH,
            ).start()
            return carry

        lax.fori_loop(0, n_dp - 1, send, 0)

    def deliver(ph):
        if ph in (0, 2):
            spread(ph, small.at[ph, 0], got.at[ph])
        else:
            spread(ph, small.at[ph, 1], mid.at[ph])

    def many(ref, sem):
        return pltpu.make_async_copy(ref, ref, sem)

    def project(x2, j, weights, w, sums):
        low, high = sums
        low = low + mm(x2, weights[w, piece * j : piece * (j + 1), :])
        high = high + mm(x2, weights[w, half + piece * j : half + piece * (j + 1), :])
        return low, high

    def branch(parts, j):
        low = high = 0.0
        for narrow, weights, w in parts:
            low = low + mm(narrow, weights[w, :, piece * j : piece * (j + 1)])
            high = high + mm(narrow, weights[w, :, half + piece * j : half + piece * (j + 1)])
        return jnp.concatenate([low[:8], high[8:]], axis=0)

    def add_branch(out, ph, x, parts, sent=None):
        for j in pieces:
            at = piece_at(j)
            out[ph, :, at] = (x[ph, :, at].astype(F32) + branch(parts, j)).astype(BF16)
            if sent is not None:
                sent(j)

    def activate(pre, w):
        logistic = 1.0 / (1.0 + jnp.exp(-pre))
        slopes[w] = logistic * (1.0 + pre * (1.0 - logistic))
        return pre * logistic

    def nothing():
        zeros = jnp.zeros((16, w_in.shape[2]), F32)
        return zeros, zeros

    def gather(sums):
        return sums[0][:8] + sums[1][8:]

    def forward_one(x, n, w):
        sums = nothing()
        for j in pieces:
            sums = project(x[n, :, piece_at(j)], j, w_in, w, sums)
        return activate(gather(sums), w)

    def forward_pair(ph, arrived, sent):
        a, b = pairs[ph]
        sums_a, sums_b = nothing(), nothing()
        for j in pieces:
            arrived(j)
            x2 = got[ph, :, piece_at(j)]
            sums_a = project(x2, j, w_in, a, sums_a)
            sums_b = project(x2, j, w_in, b, sums_b)
        act_a = activate(gather(sums_a), a)
        small[ph, 0] = act_a
        act_a = twice(act_a)
        act_b = activate(gather(sums_b) + mm(act_a, m_fwd[ph])[:8], b)
        small[ph, 1] = act_b
        parts = [(act_a, w_out, a), (twice(act_b), w_out, b)]
        add_branch(give, ph, got, parts, sent)
        return parts

    def backward_pair(ph, arrived):
        a, b = pairs[3 - ph]
        sums_a, sums_b = nothing(), nothing()
        for j in pieces:
            arrived(j)
            g2 = got[ph, :, piece_at(j)]
            sums_b = project(g2, j, t_out, b, sums_b)
            sums_a = project(g2, j, t_out, a, sums_a)
        grad_b = gather(sums_b) * slopes[b]
        small[ph, 0] = grad_b
        grad_b = twice(grad_b)
        grad_a = (gather(sums_a) + mm(grad_b, m_bwd[3 - ph])[:8]) * slopes[a]
        small[ph, 1] = grad_a
        return [(grad_b, t_in, b), (twice(grad_a), t_in, a)]

    def between(blk):
        a, b = pairs[blk]
        both = mm(w_out[a], w_in[b])
        m_fwd[blk] = both.astype(BF16)
        m_bwd[blk] = both.T.astype(BF16)

    def turn():
        tile = w_in.shape[2]

        def one(n, carry):
            w, at = n // (2 * half // tile), n % (2 * half // tile)
            at = pl.ds(pl.multiple_of(at * tile, tile), tile)
            t_in[w, :, at] = w_in[w, at, :].T
            t_out[w, at, :] = w_out[w, :, at].T
            return carry

        lax.fori_loop(0, 4 * (2 * half // tile), one, 0)

    def unpack(c, kind):
        many(rbuf.at[c, kind, pl.ds(0, n_dp - 1)], x_recv.at[c, kind]).wait()
        rows = rbuf[c, kind].astype(F32)
        flat = lambda part: part.reshape(n_dp * 8, 128)
        narrow = jnp.concatenate([flat(rows[:, 0:8]), flat(rows[:, 8:16])], axis=1)
        broad = jnp.where(path == 0, flat(rows[:, 16:24]), flat(rows[:, 24:32]))
        return narrow.astype(BF16), broad

    def prepare():
        for c in (0, 1):
            act, x = unpack(c, 0)
            act_rows[c] = act
            x_turned[c] = x.T.astype(BF16)

    def finish(c):
        grad_pre, grad_y = unpack(c, 1)
        gin_ref[0, c] = mm(x_turned[c], grad_pre)[:share]
        gout_ref[0, c] = mm(grad_y.T.astype(BF16), act_rows[c])[:share]

    early = 1 - chip // (chips // 2)

    def seeds():
        all_rows.wait()
        own = lax.broadcasted_iota(jnp.int32, (16, 128), 0) + 8 * block
        every = lax.broadcasted_iota(jnp.int32, (128, 128), 0)

        def count(group, total):
            left, right = [], []
            for n in range(8):
                tile = ids_all[group * 8 + n]
                events = jnp.where(path == 0, tile[0:1, :], tile[1:2, :])
                left.append(jnp.where(own == events, 1.0, 0.0).astype(BF16))
                right.append(jnp.where(every == tile[2:3, :], 1.0, 0.0).astype(BF16))
            return total + mm_t(jnp.concatenate(left, axis=1), jnp.concatenate(right, axis=1))

        counts = lax.fori_loop(0, n_dp // 8, count, jnp.zeros((16, 128), F32))[:8]
        sixteens = jnp.floor(counts * 0.0625)
        parts = jnp.concatenate([sixteens, counts - 16.0 * sixteens], axis=0).astype(BF16)
        sums = mm(parts, cand_ref[...])
        got[2] = fold((16.0 * sums[:8] + sums[8:]) * scale).astype(BF16)

    @pl.when(relay & (k == 0))
    def _():
        own_rows.wait()
        rows = first_rows[...].astype(F32)
        mine = jnp.where(block % 2 == 0, rows[:8], rows[8:])
        got[0] = fold(mine).astype(BF16)
        for copy in load(c1):
            copy.wait()
        act = forward_one(got, 0, c1)
        small[0, 0] = act
        add_branch(mid, 0, got, [(twice(act), w_out, c1)])

    pl.semaphore_wait(barrier, n_dp + 2)

    @pl.when(jnp.logical_not(relay))
    def _():
        @pl.when(k == 0)
        def _():
            for copy in load(c1):
                copy.wait()
            mail(0)[0].wait_recv()
            act = forward_one(mail_big, 0, c1)
            mail_small[0] = act
            add_branch(
                give,
                0,
                mail_big,
                [(twice(act), w_out, c1)],
                lambda j: hop(0, j, up_first).start(),
            )
            back().start()

        for copy in lend(c1):
            copy.start()

        @pl.when(edge)
        def _():
            spread_ids()

        for copy in lend(c1):
            copy.wait_send()
        for copy in lend(c2):
            copy.start()

        @pl.when(k > 0)
        def _():
            for copy in mail(0):
                copy.wait_recv()

        spread(0, mail_small.at[0], mail_big.at[0])
        for ph in (1, 2):
            for copy in mail(ph):
                copy.wait_recv()
            spread(ph, mail_small.at[ph], mail_big.at[ph])
        prepare()

        @pl.when(k == 0)
        def _():
            finish(early)

        for copy in mail(3):
            copy.wait_recv()
        spread(3, mail_small.at[3], mail_big.at[3])

        @pl.when(k > 0)
        def _():
            finish(early)

        finish(1 - early)
        for copy in lend(c2):
            copy.wait_send()

        @pl.when(k == 0)
        def _():
            for j in pieces:
                hop(0, j, up_first).wait_send()
            back().wait_send()

        @pl.when(edge)
        def _():
            many(ids_all.at[pl.ds(0, n_dp - 1)], ids_recv).wait()

    @pl.when(relay)
    def _():
        def from_below(ph):
            def wait(j):
                @pl.when(k > 0)
                def _():
                    hop(ph, j, down).wait_recv()

            return wait

        def from_above(ph):
            def wait(j):
                @pl.when(k < last)
                def _():
                    hop(ph, j, up).wait_recv()

            return wait

        def to_above(ph):
            def send(j):
                @pl.when(k < last)
                def _():
                    hop(ph, j, up).start()

            return send

        def to_below(ph):
            def send(j):
                @pl.when(k > 0)
                def _():
                    hop(ph, j, down).start()

            return send

        def lent(blk):
            for copy in lend((c1, c2)[blk]):
                copy.wait_recv()

        def post(ph):
            for copy in mail(ph):
                copy.start()

        @pl.when(k == 0)
        def _():
            mail(0)[0].start()
            spread_ids()
            deliver(0)
            lent(0)
            between(0)
            for copy in load(c2):
                copy.wait()
            lent(1)
            between(1)
            turn()
            many(ids_all.at[pl.ds(0, n_dp - 1)], ids_recv).wait()
            seeds()
            back().wait_recv()

        @pl.when(k > 0)
        def _():
            for copy in load(c1):
                copy.wait()
            lent(0)
            between(0)

            @pl.when(k == last)
            def _():
                for copy in load(c2):
                    copy.wait()
                lent(1)
                between(1)

            parts = forward_pair(0, from_below(0), to_above(0))
            add_branch(mid, 0, got, parts[:1])
            post(0)

            @pl.when(k == last)
            def _():
                got[1] = give[0]

            @pl.when(k < last)
            def _():
                deliver(0)
                for copy in load(c2):
                    copy.wait()
                lent(1)
                between(1)

                @pl.when(k < chips // 2)
                def _():
                    turn()

        parts = forward_pair(1, from_above(1), to_below(1))
        post(1)
        add_branch(mid, 1, got, parts[:1])

        @pl.when(k > 0)
        def _():
            deliver(1)

            @pl.when(k == last)
            def _():
                deliver(0)

            @pl.when(k >= chips // 2)
            def _():
                turn()

        parts = backward_pair(2, from_below(2))
        add_branch(give, 2, got, parts, to_above(2))
        add_branch(mid, 2, got, parts[:1])
        post(2)

        @pl.when(k < last)
        def _():
            @pl.when(k == 0)
            def _():
                deliver(1)

            deliver(2)
            prepare()

            @pl.when(k == 0)
            def _():
                finish(early)

        @pl.when(k == last)
        def _():
            got[3] = give[2]

        parts = backward_pair(3, from_above(3))

        @pl.when(k > 0)
        def _():
            add_branch(give, 3, got, parts, to_below(3))

        post(3)
        add_branch(mid, 3, got, parts[:1])
        deliver(3)

        @pl.when(k == last)
        def _():
            deliver(2)
            prepare()

        @pl.when(k > 0)
        def _():
            finish(early)

        finish(1 - early)

        @pl.when(k < last)
        def _():
            for j in pieces:
                hop(2, j, up).wait_send()

        @pl.when((k > 0) & (k < last))
        def _():
            for j in pieces:
                hop(0, j, up).wait_send()

        @pl.when(k > 0)
        def _():
            for j in pieces:
                hop(1, j, down).wait_send()
                hop(3, j, down).wait_send()
            mail(0)[1].wait_send()

        mail(0)[0].wait_send()
        for ph in (1, 2, 3):
            for copy in mail(ph):
                copy.wait_send()

    @pl.when(edge)
    def _():
        many(ids_all.at[pl.ds(0, n_dp - 1)], ids_send).wait()

    for c in (0, 1):
        for kind in (0, 1):
            many(rbuf.at[c, kind, pl.ds(0, n_dp - 1)], x_send.at[c, kind]).wait()


def local(n_pipe, n_dp, item_ids, plan_order, candidates, adapters_in, adapters_out):
    batches, width = item_ids.shape
    events = width - 1
    _, _, features, hidden = adapters_in.shape
    share = features // n_dp
    scale = 1.0 / math.sqrt(batches * n_dp * events)
    plan = jnp.pad(plan_order, (0, item_ids.shape[1] - plan_order.shape[0]))
    ids = jnp.concatenate([item_ids, plan[None]], axis=0)
    vmem = pl.BlockSpec(memory_space=pltpu.VMEM)
    hbm = pl.BlockSpec(memory_space=pltpu.HBM)
    grad_in, grad_out = pl.pallas_call(
        functools.partial(kernel, n_pipe, n_dp, scale),
        out_shape=(
            jax.ShapeDtypeStruct((1, 2, share, hidden), F32),
            jax.ShapeDtypeStruct((1, 2, share, hidden), F32),
        ),
        in_specs=[hbm] * 4,
        out_specs=(vmem, vmem),
        scratch_shapes=[
            pltpu.VMEM((4, features, hidden), BF16),
            pltpu.VMEM((4, hidden, features), BF16),
            pltpu.VMEM((4, hidden, features), BF16),
            pltpu.VMEM((4, features, hidden), BF16),
            pltpu.VMEM((2, hidden, hidden), BF16),
            pltpu.VMEM((2, hidden, hidden), BF16),
            pltpu.VMEM(ids.shape, jnp.int32),
            pltpu.VMEM(candidates.shape, BF16),
            pltpu.VMEM((16, features), BF16),
            pltpu.VMEM((8, 128), jnp.int32),
            pltpu.VMEM((n_dp, 8, 128), jnp.int32),
            pltpu.VMEM((4, 16, features // 2), BF16),
            pltpu.VMEM((4, 16, features // 2), BF16),
            pltpu.VMEM((4, 16, features // 2), BF16),
            pltpu.VMEM((4, 2, 8, hidden), F32),
            pltpu.VMEM((4, 8, hidden), F32),
            pltpu.VMEM((4, 16, features // 2), BF16),
            pltpu.VMEM((4, 8, hidden), F32),
            pltpu.VMEM((2, 2, n_dp // 2, 32, 128), BF16),
            pltpu.VMEM((2, 2, n_dp, 32, 128), BF16),
            pltpu.VMEM((2, 128, n_dp * 8), BF16),
            pltpu.VMEM((2, n_dp * 8, hidden), BF16),
            pltpu.SemaphoreType.DMA((2, 2)),
            pltpu.SemaphoreType.DMA((3,)),
            pltpu.SemaphoreType.DMA((2, 2)),
            pltpu.SemaphoreType.DMA((2, 2)),
            pltpu.SemaphoreType.DMA((4, PIECES)),
            pltpu.SemaphoreType.DMA((4, PIECES)),
            pltpu.SemaphoreType.DMA((4, 2)),
            pltpu.SemaphoreType.DMA((4, 2)),
            pltpu.SemaphoreType.DMA,
            pltpu.SemaphoreType.DMA,
            pltpu.SemaphoreType.DMA,
            pltpu.SemaphoreType.DMA,
            pltpu.SemaphoreType.DMA((2, 2)),
            pltpu.SemaphoreType.DMA((2, 2)),
        ],
        compiler_params=pltpu.CompilerParams(
            collective_id=0, has_side_effects=True, vmem_limit_bytes=107 * 512 * 1024
        ),
    )(ids, candidates, adapters_in, adapters_out)
    return grad_in, jnp.swapaxes(grad_out, 2, 3)


def solution(mesh):
    in_specs = (P(None, "dp"), P(), P(), P("pipe", None, None, None), P("pipe", None, None, None))
    out_specs = (P("pipe", None, "dp", None), P("pipe", None, None, "dp"))
    return jax.shard_map(
        functools.partial(local, mesh.shape["pipe"], mesh.shape["dp"]),
        mesh=mesh,
        in_specs=in_specs,
        out_specs=out_specs,
        check_vma=False,
    )
```

```python
import functools
import math

import jax
import jax.numpy as jnp
from jax import lax
from jax.experimental import pallas as pl
from jax.experimental.pallas import tpu as pltpu
from jax.sharding import PartitionSpec as P

MESH = pl.DeviceIdType.MESH
F32 = jnp.float32
BF16 = jnp.bfloat16
PIECES = 3


def mm(a, b):
    return jnp.dot(a, b, preferred_element_type=F32)


def mm_t(a, b):
    return lax.dot_general(a, b, (((1,), (1,)), ((), ())), preferred_element_type=F32)


def t_mm(a, b):
    return lax.dot_general(a, b, (((0,), (0,)), ((), ())), preferred_element_type=F32)


def fold(wide):
    half = wide.shape[1] // 2
    return jnp.concatenate([wide[:, :half], wide[:, half:]], axis=0)


def twice(rows):
    return jnp.concatenate([rows, rows], axis=0).astype(BF16)


def kernel(
    n_pipe,
    n_dp,
    scale,
    ids_hbm,
    cand_hbm,
    win_ref,
    wout_ref,
    gin_ref,
    gout_ref,
    w_in,
    w_out,
    t_in,
    t_out,
    m_fwd,
    m_bwd,
    ids_ref,
    cand_ref,
    first_rows,
    ids_own,
    ids_all,
    xs,
    give,
    small,
    slopes,
    sbuf,
    rbuf,
    x_turned,
    act_rows,
    w_sem,
    cand_sem,
    share_send,
    share_recv,
    give_sem,
    got_sem,
    mail_send,
    mail_recv,
    pass_send,
    pass_recv,
    back_send,
    back_recv,
    ids_send,
    ids_recv,
    x_send,
    x_recv,
):
    p = lax.axis_index("pipe")
    d = lax.axis_index("dp")
    half_dp = n_dp // 2
    path = d // half_dp
    block = d % half_dp
    c1 = path
    c2 = 1 - path
    chips = n_pipe // 2
    chip = p // 2
    core = p % 2
    relay = core == 1
    starts = core == path
    other = p + 1 - 2 * core
    last = chips - 1
    k = chip + path * (last - 2 * chip)
    up = 2 * chip + 3 - 4 * path
    down = 2 * chip - 1 + 4 * path
    edge = (k == 0) | (k == last)
    half = w_in.shape[1] // 2
    n_items = cand_ref.shape[0]
    piece = half // PIECES
    pieces = range(PIECES)
    pairs = ((c1 + 2 - 2 * path, c1 + 2 * path), (c2 + 2 * path, c2 + 2 - 2 * path))

    def own(ph):
        return (ph + 1 + path) % 2

    share = 2 * half // n_dp
    cs = (c1, c2, c2, c1)

    def load(c):
        return (
            pltpu.make_async_copy(win_ref.at[0, c], w_in.at[c], w_sem.at[c, 0]),
            pltpu.make_async_copy(wout_ref.at[0, c], w_out.at[c], w_sem.at[c, 1]),
        )

    def lend(c):
        return [
            pltpu.make_async_remote_copy(
                src_ref=src.at[0, c],
                dst_ref=dst.at[2 + c],
                send_sem=share_send.at[c, n],
                recv_sem=share_recv.at[c, n],
                device_id={"pipe": other},
                device_id_type=MESH,
            )
            for n, (src, dst) in enumerate(((win_ref, w_in), (wout_ref, w_out)))
        ]

    start = pl.multiple_of(16 * (block // 2), 16)
    own_rows = pltpu.make_async_copy(cand_hbm.at[pl.ds(start, 16)], first_rows, cand_sem.at[0])
    all_rows = pltpu.make_async_copy(cand_hbm, cand_ref, cand_sem.at[1])

    id_copy = pltpu.make_async_copy(ids_hbm, ids_ref, cand_sem.at[2])

    @pl.when(starts & (k == 0))
    def _():
        own_rows.start()

    @pl.when(relay | (k == 0))
    def _():
        for copy in load(c1):
            copy.start()

    @pl.when(relay)
    def _():
        @pl.when(edge)
        def _():
            id_copy.start()

        for copy in load(c2):
            copy.start()

        @pl.when(k == 0)
        def _():
            all_rows.start()

    barrier = pltpu.get_barrier_semaphore()

    def hello(to):
        pl.semaphore_signal(barrier, inc=1, device_id={"pipe": to}, device_id_type=MESH)

    hello(other)

    @pl.when(relay & (k < last))
    def _():
        hello(up)

    @pl.when(relay & (k > 0))
    def _():
        hello(down)

    def greet(n, carry):
        pl.semaphore_signal(
            barrier, inc=1, device_id={"dp": lax.rem(d + n, n_dp)}, device_id_type=MESH
        )
        return carry

    lax.fori_loop(1, n_dp, greet, 0)

    def far_first(n):
        side = d // 16, (d // 4) % 4, d % 4

        def away(t):
            return (2 + 3 * (t * (t + 1) // 2)) % 4

        plane = (side[0] + 1 - n % 2) % 2
        column = (side[1] + away(n // 8)) % 4
        return 16 * plane + 4 * column + (side[2] + away((n // 2) % 4)) % 4

    def piece_at(j):
        return pl.ds(j * piece, piece)

    def hop(ph, j, to):
        return pltpu.make_async_remote_copy(
            src_ref=give.at[ph, :, piece_at(j)],
            dst_ref=xs.at[ph, 0, :, piece_at(j)],
            send_sem=give_sem.at[ph, j],
            recv_sem=got_sem.at[ph, j],
            device_id={"pipe": to},
            device_id_type=MESH,
        )

    def back():
        return pltpu.make_async_remote_copy(
            src_ref=slopes.at[c1],
            dst_ref=slopes.at[2 + c1],
            send_sem=back_send,
            recv_sem=back_recv,
            device_id={"pipe": other},
            device_id_type=MESH,
        )

    def pass_on():
        return pltpu.make_async_remote_copy(
            src_ref=xs.at[0, 1],
            dst_ref=xs.at[0, 1],
            send_sem=pass_send,
            recv_sem=pass_recv,
            device_id={"pipe": other},
            device_id_type=MESH,
        )

    def mail(ph):
        n = 1 - own(ph)
        return [
            pltpu.make_async_remote_copy(
                src_ref=ref.at[ph, n],
                dst_ref=ref.at[ph, n],
                send_sem=mail_send.at[ph, m],
                recv_sem=mail_recv.at[ph, m],
                device_id={"pipe": other},
                device_id_type=MESH,
            )
            for m, ref in enumerate((xs, small))
        ]

    def spread_ids():
        id_copy.wait()
        lane = lax.broadcasted_iota(jnp.int32, (1, 128), 1)
        front = back = target = jnp.full((1, 128), -1, jnp.int32)
        ids_own[...] = jnp.full((8, 128), -1, jnp.int32)
        ids_own[0:4, 0:33] = ids_ref[...]
        for m in range(4):
            row = ids_own[m : m + 1, :]
            is_front = row < 2 * n_items
            for above in (2 * n_items, n_items):
                row = jnp.where(row >= above, row - above, row)
            fronts = jnp.where(is_front, row, -1)
            backs = jnp.where(is_front, -1, row)
            here = lane // 32 == m
            front = jnp.where(here, pltpu.roll(fronts, 32 * m, 1) if m else fronts, front)
            back = jnp.where(here, pltpu.roll(backs, 32 * m, 1) if m else backs, back)
            target = jnp.where(here, pltpu.roll(row, (32 * m + 127) % 128, 1), target)
        ids_own[0:1, :] = front
        ids_own[1:2, :] = back
        ids_own[2:3, :] = target
        ids_all[d] = ids_own[...]

        def send(n, carry):
            pltpu.make_async_remote_copy(
                src_ref=ids_own,
                dst_ref=ids_all.at[d],
                send_sem=ids_send,
                recv_sem=ids_recv,
                device_id={"dp": lax.rem(d + n, n_dp)},
                device_id_type=MESH,
            ).start()
            return carry

        lax.fori_loop(1, n_dp, send, 0)

    def spread(ph, narrow, broad):
        c, kind = cs[ph], ph // 2
        narrow, broad = narrow[...], broad[...].astype(F32)
        hidden = narrow.shape[1] // 2
        top = jnp.concatenate([narrow[:, :hidden], narrow[:, hidden:]], axis=0).astype(BF16)
        wide = jnp.concatenate([broad, broad[:, :128]], axis=1)
        for j in range(half_dp):
            sbuf[c, kind, j, 0:16, :] = top
            sbuf[c, kind, j, 16:32, :] = wide[:, share * j : share * j + 128].astype(BF16)
        rbuf[c, kind, d] = sbuf[c, kind, block]

        def send(n, carry):
            peer = far_first(n)
            pltpu.make_async_remote_copy(
                src_ref=sbuf.at[c, kind, lax.rem(peer, half_dp)],
                dst_ref=rbuf.at[c, kind, d],
                send_sem=x_send.at[c, kind],
                recv_sem=x_recv.at[c, kind],
                device_id={"dp": peer},
                device_id_type=MESH,
            ).start()
            return carry

        lax.fori_loop(0, n_dp - 1, send, 0)

    def deliver(ph, n):
        spread(ph, small.at[ph, n], xs.at[ph, n])

    def many(ref, sem):
        return pltpu.make_async_copy(ref, ref, sem)

    def project(x2, j, weights, w, sums):
        low, high = sums
        low = low + mm(x2, weights[w, piece * j : piece * (j + 1), :])
        high = high + mm(x2, weights[w, half + piece * j : half + piece * (j + 1), :])
        return low, high

    def branch(parts, j):
        low = high = 0.0
        for narrow, weights, w in parts:
            low = low + mm(narrow, weights[w, :, piece * j : piece * (j + 1)])
            high = high + mm(narrow, weights[w, :, half + piece * j : half + piece * (j + 1)])
        return jnp.concatenate([low[:8], high[8:]], axis=0)

    def add_branch(out, x, parts, sent=None):
        for j in pieces:
            at = piece_at(j)
            out[:, at] = (x[:, at].astype(F32) + branch(parts, j)).astype(BF16)
            if sent is not None:
                sent(j)

    def activate(pre, w):
        logistic = 1.0 / (1.0 + jnp.exp(-pre))
        slopes[w] = logistic * (1.0 + pre * (1.0 - logistic))
        return pre * logistic

    def nothing():
        zeros = jnp.zeros((16, w_in.shape[2]), F32)
        return zeros, zeros

    def gather(sums):
        return sums[0][:8] + sums[1][8:]

    def forward_one(n):
        sums = nothing()
        for j in pieces:
            sums = project(xs[0, n, :, piece_at(j)], j, w_in, c1, sums)
        act = activate(gather(sums), c1)
        small[0, n] = act
        return [(twice(act), w_out, c1)]

    def forward_pair(ph, arrived, sent):
        a, b = pairs[ph]
        sums_a, sums_b = nothing(), nothing()
        for j in pieces:
            arrived(j)
            x2 = xs[ph, 0, :, piece_at(j)]
            sums_a = project(x2, j, w_in, a, sums_a)
            sums_b = project(x2, j, w_in, b, sums_b)
        act_a = activate(gather(sums_a), a)
        small[ph, 0] = act_a
        act_a = twice(act_a)
        act_b = activate(gather(sums_b) + mm(act_a, m_fwd[ph])[:8], b)
        small[ph, 1] = act_b
        parts = [(act_a, w_out, a), (twice(act_b), w_out, b)]
        add_branch(give.at[ph], xs.at[ph, 0], parts, sent)
        return parts

    def backward_pair(ph, arrived):
        a, b = pairs[3 - ph]
        sums_a, sums_b = nothing(), nothing()
        for j in pieces:
            arrived(j)
            g2 = xs[ph, 0, :, piece_at(j)]
            sums_b = project(g2, j, t_out, b, sums_b)
            sums_a = project(g2, j, t_out, a, sums_a)
        grad_b = gather(sums_b) * slopes[b]
        small[ph, 0] = grad_b
        grad_b = twice(grad_b)
        grad_a = (gather(sums_a) + mm(grad_b, m_bwd[3 - ph])[:8]) * slopes[a]
        small[ph, 1] = grad_a
        return [(grad_b, t_in, b), (twice(grad_a), t_in, a)]

    def between(blk):
        a, b = pairs[blk]
        both = mm(w_out[a], w_in[b])
        m_fwd[blk] = both.astype(BF16)
        m_bwd[blk] = both.T.astype(BF16)

    def turn():
        tile = w_in.shape[2]

        def one(n, carry):
            w, at = n // (2 * half // tile), n % (2 * half // tile)
            at = pl.ds(pl.multiple_of(at * tile, tile), tile)
            t_in[w, :, at] = w_in[w, at, :].T
            t_out[w, at, :] = w_out[w, :, at].T
            return carry

        lax.fori_loop(0, 4 * (2 * half // tile), one, 0)

    def unpack(c, kind):
        many(rbuf.at[c, kind, pl.ds(0, n_dp - 1)], x_recv.at[c, kind]).wait()
        rows = rbuf[c, kind].astype(F32)
        flat = lambda part: part.reshape(n_dp * 8, 128)
        narrow = jnp.concatenate([flat(rows[:, 0:8]), flat(rows[:, 8:16])], axis=1)
        broad = jnp.where(path == 0, flat(rows[:, 16:24]), flat(rows[:, 24:32]))
        return narrow.astype(BF16), broad

    def prepare():
        for c in (0, 1):
            act, x = unpack(c, 0)
            act_rows[c] = act
            x_turned[c] = x.T.astype(BF16)

    def finish(c):
        grad_pre, grad_y = unpack(c, 1)
        gin_ref[0, c] = mm(x_turned[c], grad_pre)[:share]
        gout_ref[0, c] = mm(grad_y.T.astype(BF16), act_rows[c])[:share]

    early = 1 - chip // (chips // 2)

    def seeds():
        all_rows.wait()
        mine = lax.broadcasted_iota(jnp.int32, (16, 128), 0) + 8 * block
        every = lax.broadcasted_iota(jnp.int32, (128, 128), 0)

        def count(group, total):
            left, right = [], []
            for n in range(8):
                tile = ids_all[group * 8 + n]
                events = jnp.where(path == 0, tile[0:1, :], tile[1:2, :])
                left.append(jnp.where(mine == events, 1.0, 0.0).astype(BF16))
                right.append(jnp.where(every == tile[2:3, :], 1.0, 0.0).astype(BF16))
            return total + mm_t(jnp.concatenate(left, axis=1), jnp.concatenate(right, axis=1))

        counts = lax.fori_loop(0, n_dp // 8, count, jnp.zeros((16, 128), F32))[:8]
        sixteens = jnp.floor(counts * 0.0625)
        parts = jnp.concatenate([sixteens, counts - 16.0 * sixteens], axis=0).astype(BF16)
        sums = mm(parts, cand_ref[...])
        xs[2, 0] = fold((16.0 * sums[:8] + sums[8:]) * scale).astype(BF16)

    @pl.when(starts & (k == 0))
    def _():
        own_rows.wait()
        rows = first_rows[...].astype(F32)
        mine = jnp.where(block % 2 == 0, rows[:8], rows[8:])
        xs[0, 0] = fold(mine).astype(BF16)
        for copy in load(c1):
            copy.wait()
        add_branch(xs.at[0, 1], xs.at[0, 0], forward_one(0))

    @pl.when(relay & (k > 0) & (k < last))
    def _():
        pl.semaphore_wait(barrier, n_dp + 2)

    @pl.when(relay & edge)
    def _():
        pl.semaphore_wait(barrier, n_dp + 1)

    @pl.when(jnp.logical_not(relay))
    def _():
        pl.semaphore_wait(barrier, n_dp)

    @pl.when(k == 0)
    def _():
        @pl.when(starts)
        def _():
            pass_on().start()

        @pl.when(jnp.logical_not(starts))
        def _():
            for copy in load(c1):
                copy.wait()
            pass_on().wait_recv()
            add_branch(
                give.at[0], xs.at[0, 1], forward_one(1), lambda j: hop(0, j, up).start()
            )

    @pl.when(jnp.logical_not(relay))
    def _():
        @pl.when(k == 0)
        def _():
            back().start()

        for copy in lend(c1):
            copy.start()
        for copy in lend(c1):
            copy.wait_send()
        for copy in lend(c2):
            copy.start()

        @pl.when(k > 0)
        def _():
            for copy in mail(0):
                copy.wait_recv()

        deliver(0, 1 - own(0))
        for ph in (1, 2):
            for copy in mail(ph):
                copy.wait_recv()
            deliver(ph, 1 - own(ph))
        prepare()

        @pl.when(k == 0)
        def _():
            finish(early)

        for copy in mail(3):
            copy.wait_recv()
        deliver(3, 1 - own(3))

        @pl.when(k > 0)
        def _():
            finish(early)

        finish(1 - early)
        for copy in lend(c2):
            copy.wait_send()

        @pl.when(k == 0)
        def _():
            back().wait_send()

    @pl.when(relay)
    def _():
        def from_below(ph):
            def wait(j):
                @pl.when(k > 0)
                def _():
                    hop(ph, j, down).wait_recv()

            return wait

        def from_above(ph):
            def wait(j):
                @pl.when(k < last)
                def _():
                    hop(ph, j, up).wait_recv()

            return wait

        def to_above(ph):
            def send(j):
                @pl.when(k < last)
                def _():
                    hop(ph, j, up).start()

            return send

        def to_below(ph):
            def send(j):
                @pl.when(k > 0)
                def _():
                    hop(ph, j, down).start()

            return send

        def lent(blk):
            for copy in lend((c1, c2)[blk]):
                copy.wait_recv()

        def post(ph):
            for copy in mail(ph):
                copy.start()

        @pl.when(k == 0)
        def _():
            spread_ids()
            deliver(0, own(0))
            lent(0)
            between(0)
            for copy in load(c2):
                copy.wait()
            lent(1)
            between(1)
            turn()
            many(ids_all.at[pl.ds(0, n_dp - 1)], ids_recv).wait()
            seeds()
            back().wait_recv()

        @pl.when(k > 0)
        def _():
            for copy in load(c1):
                copy.wait()
            lent(0)
            between(0)

            @pl.when(k == last)
            def _():
                spread_ids()
                for copy in load(c2):
                    copy.wait()
                lent(1)
                between(1)

            parts = forward_pair(0, from_below(0), to_above(0))
            add_branch(xs.at[0, 1], xs.at[0, 0], parts[:1])
            post(0)

            @pl.when(k == last)
            def _():
                xs[1, 0] = give[0]

            @pl.when(k < last)
            def _():
                deliver(0, own(0))
                for copy in load(c2):
                    copy.wait()
                lent(1)
                between(1)

                @pl.when(k < chips // 2)
                def _():
                    turn()

        parts = forward_pair(1, from_above(1), to_below(1))
        add_branch(xs.at[1, 1], xs.at[1, 0], parts[:1])
        post(1)

        @pl.when(k > 0)
        def _():
            deliver(1, own(1))

            @pl.when(k == last)
            def _():
                deliver(0, own(0))

            @pl.when(k >= chips // 2)
            def _():
                turn()

        parts = backward_pair(2, from_below(2))
        add_branch(give.at[2], xs.at[2, 0], parts, to_above(2))
        add_branch(xs.at[2, 1], xs.at[2, 0], parts[:1])
        post(2)

        @pl.when(k < last)
        def _():
            @pl.when(k == 0)
            def _():
                deliver(1, own(1))

            deliver(2, own(2))
            prepare()

            @pl.when(k == 0)
            def _():
                finish(early)

        @pl.when(k == last)
        def _():
            xs[3, 0] = give[2]

        parts = backward_pair(3, from_above(3))

        @pl.when(k > 0)
        def _():
            add_branch(give.at[3], xs.at[3, 0], parts, to_below(3))

        add_branch(xs.at[3, 1], xs.at[3, 0], parts[:1])
        post(3)
        deliver(3, own(3))

        @pl.when(k == last)
        def _():
            deliver(2, own(2))
            prepare()

        @pl.when(k > 0)
        def _():
            finish(early)

        finish(1 - early)

        @pl.when(k < last)
        def _():
            for j in pieces:
                hop(2, j, up).wait_send()

        @pl.when((k > 0) & (k < last))
        def _():
            for j in pieces:
                hop(0, j, up).wait_send()

        @pl.when(k > 0)
        def _():
            for j in pieces:
                hop(1, j, down).wait_send()
                hop(3, j, down).wait_send()
            for copy in mail(0):
                copy.wait_send()

        for ph in (1, 2, 3):
            for copy in mail(ph):
                copy.wait_send()

        @pl.when(k == last)
        def _():
            many(ids_all.at[pl.ds(0, n_dp - 1)], ids_recv).wait()

        @pl.when(edge)
        def _():
            many(ids_all.at[pl.ds(0, n_dp - 1)], ids_send).wait()

    @pl.when(k == 0)
    def _():
        @pl.when(starts)
        def _():
            pass_on().wait_send()

        @pl.when(jnp.logical_not(starts))
        def _():
            for j in pieces:
                hop(0, j, up).wait_send()

    for c in (0, 1):
        for kind in (0, 1):
            many(rbuf.at[c, kind, pl.ds(0, n_dp - 1)], x_send.at[c, kind]).wait()


def local(n_pipe, n_dp, item_ids, plan_order, candidates, adapters_in, adapters_out):
    batches, width = item_ids.shape
    events = width - 1
    _, _, features, hidden = adapters_in.shape
    share = features // n_dp
    scale = 1.0 / math.sqrt(batches * n_dp * events)
    ids = item_ids + candidates.shape[0] * plan_order[:, None]
    vmem = pl.BlockSpec(memory_space=pltpu.VMEM)
    hbm = pl.BlockSpec(memory_space=pltpu.HBM)
    grad_in, grad_out = pl.pallas_call(
        functools.partial(kernel, n_pipe, n_dp, scale),
        out_shape=(
            jax.ShapeDtypeStruct((1, 2, share, hidden), F32),
            jax.ShapeDtypeStruct((1, 2, share, hidden), F32),
        ),
        in_specs=[hbm] * 4,
        out_specs=(vmem, vmem),
        scratch_shapes=[
            pltpu.VMEM((4, features, hidden), BF16),
            pltpu.VMEM((4, hidden, features), BF16),
            pltpu.VMEM((4, hidden, features), BF16),
            pltpu.VMEM((4, features, hidden), BF16),
            pltpu.VMEM((2, hidden, hidden), BF16),
            pltpu.VMEM((2, hidden, hidden), BF16),
            pltpu.VMEM(ids.shape, jnp.int32),
            pltpu.VMEM(candidates.shape, BF16),
            pltpu.VMEM((16, features), BF16),
            pltpu.VMEM((8, 128), jnp.int32),
            pltpu.VMEM((n_dp, 8, 128), jnp.int32),
            pltpu.VMEM((4, 2, 16, features // 2), BF16),
            pltpu.VMEM((4, 16, features // 2), BF16),
            pltpu.VMEM((4, 2, 8, hidden), F32),
            pltpu.VMEM((4, 8, hidden), F32),
            pltpu.VMEM((2, 2, n_dp // 2, 32, 128), BF16),
            pltpu.VMEM((2, 2, n_dp, 32, 128), BF16),
            pltpu.VMEM((2, 128, n_dp * 8), BF16),
            pltpu.VMEM((2, n_dp * 8, hidden), BF16),
            pltpu.SemaphoreType.DMA((2, 2)),
            pltpu.SemaphoreType.DMA((3,)),
            pltpu.SemaphoreType.DMA((2, 2)),
            pltpu.SemaphoreType.DMA((2, 2)),
            pltpu.SemaphoreType.DMA((4, PIECES)),
            pltpu.SemaphoreType.DMA((4, PIECES)),
            pltpu.SemaphoreType.DMA((4, 2)),
            pltpu.SemaphoreType.DMA((4, 2)),
            pltpu.SemaphoreType.DMA,
            pltpu.SemaphoreType.DMA,
            pltpu.SemaphoreType.DMA,
            pltpu.SemaphoreType.DMA,
            pltpu.SemaphoreType.DMA,
            pltpu.SemaphoreType.DMA,
            pltpu.SemaphoreType.DMA((2, 2)),
            pltpu.SemaphoreType.DMA((2, 2)),
        ],
        compiler_params=pltpu.CompilerParams(
            collective_id=0, has_side_effects=True, vmem_limit_bytes=107 * 512 * 1024
        ),
    )(ids, candidates, adapters_in, adapters_out)
    return grad_in, jnp.swapaxes(grad_out, 2, 3)


def solution(mesh):
    in_specs = (P(None, "dp"), P(), P(), P("pipe", None, None, None), P("pipe", None, None, None))
    out_specs = (P("pipe", None, "dp", None), P("pipe", None, None, "dp"))
    return jax.shard_map(
        functools.partial(local, mesh.shape["pipe"], mesh.shape["dp"]),
        mesh=mesh,
        in_specs=in_specs,
        out_specs=out_specs,
        check_vma=False,
    )
```

```python
import functools
import math

import jax
import jax.numpy as jnp
from jax import lax
from jax.experimental import pallas as pl
from jax.experimental.pallas import tpu as pltpu
from jax.sharding import PartitionSpec as P

MESH = pl.DeviceIdType.MESH
F32 = jnp.float32
BF16 = jnp.bfloat16
PIECES = 3


def mm(a, b):
    return jnp.dot(a, b, preferred_element_type=F32)


def mm_t(a, b):
    return lax.dot_general(a, b, (((1,), (1,)), ((), ())), preferred_element_type=F32)


def t_mm(a, b):
    return lax.dot_general(a, b, (((0,), (0,)), ((), ())), preferred_element_type=F32)


def fold(wide):
    half = wide.shape[1] // 2
    return jnp.concatenate([wide[:, :half], wide[:, half:]], axis=0)


def twice(rows):
    return jnp.concatenate([rows, rows], axis=0).astype(BF16)


def kernel(
    n_pipe,
    n_dp,
    scale,
    ids_hbm,
    cand_hbm,
    win_ref,
    wout_ref,
    gin_ref,
    gout_ref,
    w_in,
    w_out,
    t_in,
    t_out,
    m_fwd,
    m_bwd,
    ids_ref,
    cand_ref,
    first_rows,
    ids_own,
    ids_all,
    xs,
    give,
    small,
    slopes,
    sbuf,
    rbuf,
    x_turned,
    act_rows,
    w_sem,
    cand_sem,
    share_send,
    share_recv,
    give_sem,
    got_sem,
    mail_send,
    mail_recv,
    pass_send,
    pass_recv,
    back_send,
    back_recv,
    ids_send,
    ids_recv,
    x_send,
    x_recv,
):
    p = lax.axis_index("pipe")
    d = lax.axis_index("dp")
    half_dp = n_dp // 2
    path = d // half_dp
    block = d % half_dp
    c1 = path
    c2 = 1 - path
    chips = n_pipe // 2
    chip = p // 2
    core = p % 2
    relay = core == 1
    starts = core == path
    other = p + 1 - 2 * core
    last = chips - 1
    k = chip + path * (last - 2 * chip)
    up = 2 * chip + 3 - 4 * path
    down = 2 * chip - 1 + 4 * path
    edge = (k == 0) | (k == last)
    half = w_in.shape[1] // 2
    n_items = cand_ref.shape[0]
    piece = half // PIECES
    pieces = range(PIECES)
    pairs = ((c1 + 2 - 2 * path, c1 + 2 * path), (c2 + 2 * path, c2 + 2 - 2 * path))

    spared = (core == 0) & (k == 0)

    def own(ph):
        return (ph + 1 + path) % 2

    share = 2 * half // n_dp
    cs = (c1, c2, c2, c1)

    def load(c):
        return (
            pltpu.make_async_copy(win_ref.at[0, c], w_in.at[c], w_sem.at[c, 0]),
            pltpu.make_async_copy(wout_ref.at[0, c], w_out.at[c], w_sem.at[c, 1]),
        )

    def lend(c):
        return [
            pltpu.make_async_remote_copy(
                src_ref=src.at[0, c],
                dst_ref=dst.at[2 + c],
                send_sem=share_send.at[c, n],
                recv_sem=share_recv.at[c, n],
                device_id={"pipe": other},
                device_id_type=MESH,
            )
            for n, (src, dst) in enumerate(((win_ref, w_in), (wout_ref, w_out)))
        ]

    start = pl.multiple_of(16 * (block // 2), 16)
    own_rows = pltpu.make_async_copy(cand_hbm.at[pl.ds(start, 16)], first_rows, cand_sem.at[0])
    all_rows = pltpu.make_async_copy(cand_hbm, cand_ref, cand_sem.at[1])

    id_copy = pltpu.make_async_copy(ids_hbm, ids_ref, cand_sem.at[2])

    @pl.when(starts & (k == 0))
    def _():
        own_rows.start()

    @pl.when(relay | (k == 0))
    def _():
        for copy in load(c1):
            copy.start()

    @pl.when(relay)
    def _():
        @pl.when(edge)
        def _():
            id_copy.start()

        for copy in load(c2):
            copy.start()

        @pl.when(k == 0)
        def _():
            all_rows.start()

    side, row, column = d // 16, (d // 4) % 4, d % 4
    planes = [16 * ((side + 1) % 2), 16 * side]
    columns = [(column + away) % 4 for away in (2, 1, 3, 0)]

    def each_peer(do, too=0):
        def line(n, carry):
            at = 4 * ((row + (2 + 3 * (n * (n + 1) // 2)) % 4) % 4)
            for x in columns:
                for z in planes:
                    do(z + at + x, at + x)
            return carry

        lax.fori_loop(0, 3, line, 0)
        near = [(z, x) for x in columns for z in planes]
        for z, x in near[: 7 + too]:
            do(z + 4 * row + x, 4 * row + x)

    barrier = pltpu.get_barrier_semaphore()

    def hello(to):
        pl.semaphore_signal(barrier, inc=1, device_id={"pipe": to}, device_id_type=MESH)

    hello(other)

    @pl.when(relay & (k < last))
    def _():
        hello(up)

    @pl.when(relay & (k > 0))
    def _():
        hello(down)

    def greet(peer, place):
        pl.semaphore_signal(barrier, inc=1, device_id={"dp": peer}, device_id_type=MESH)

    each_peer(greet)

    def piece_at(j):
        return pl.ds(j * piece, piece)

    def hop(ph, j, to):
        return pltpu.make_async_remote_copy(
            src_ref=give.at[ph, :, piece_at(j)],
            dst_ref=xs.at[ph, 0, :, piece_at(j)],
            send_sem=give_sem.at[ph, j],
            recv_sem=got_sem.at[ph, j],
            device_id={"pipe": to},
            device_id_type=MESH,
        )

    def back():
        return pltpu.make_async_remote_copy(
            src_ref=slopes.at[c1],
            dst_ref=slopes.at[2 + c1],
            send_sem=back_send,
            recv_sem=back_recv,
            device_id={"pipe": other},
            device_id_type=MESH,
        )

    def pass_on():
        return pltpu.make_async_remote_copy(
            src_ref=xs.at[0, 1],
            dst_ref=xs.at[0, 1],
            send_sem=pass_send,
            recv_sem=pass_recv,
            device_id={"pipe": other},
            device_id_type=MESH,
        )

    def mail(ph):
        n = 1 - own(ph)
        return [
            pltpu.make_async_remote_copy(
                src_ref=ref.at[ph, n],
                dst_ref=ref.at[ph, n],
                send_sem=mail_send.at[ph, m],
                recv_sem=mail_recv.at[ph, m],
                device_id={"pipe": other},
                device_id_type=MESH,
            )
            for m, ref in enumerate((xs, small))
        ]

    def spread_ids():
        id_copy.wait()
        lane = lax.broadcasted_iota(jnp.int32, (1, 128), 1)
        front = back = target = jnp.full((1, 128), -1, jnp.int32)
        ids_own[...] = jnp.full((8, 128), -1, jnp.int32)
        ids_own[0:4, 0:33] = ids_ref[...]
        for m in range(4):
            row = ids_own[m : m + 1, :]
            is_front = row < 2 * n_items
            for above in (2 * n_items, n_items):
                row = jnp.where(row >= above, row - above, row)
            fronts = jnp.where(is_front, row, -1)
            backs = jnp.where(is_front, -1, row)
            here = lane // 32 == m
            front = jnp.where(here, pltpu.roll(fronts, 32 * m, 1) if m else fronts, front)
            back = jnp.where(here, pltpu.roll(backs, 32 * m, 1) if m else backs, back)
            target = jnp.where(here, pltpu.roll(row, (32 * m + 127) % 128, 1), target)
        ids_own[0:1, :] = front
        ids_own[1:2, :] = back
        ids_own[2:3, :] = target
        ids_all[d] = ids_own[...]

        def send(peer, place):
            pltpu.make_async_remote_copy(
                src_ref=ids_own,
                dst_ref=ids_all.at[d],
                send_sem=ids_send,
                recv_sem=ids_recv,
                device_id={"dp": peer},
                device_id_type=MESH,
            ).start()

        each_peer(send)

    def spread(ph, n, for_other=False):
        c, kind = cs[ph], ph // 2
        box = 2 if for_other else c
        narrow, broad = small.at[ph, n], xs.at[ph, n]
        narrow, broad = narrow[...], broad[...].astype(F32)
        hidden = narrow.shape[1] // 2
        top = jnp.concatenate([narrow[:, :hidden], narrow[:, hidden:]], axis=0).astype(BF16)
        wide = jnp.concatenate([broad, broad[:, :128]], axis=1)
        for j in range(half_dp):
            sbuf[box, kind, j, 0:16, :] = top
            sbuf[box, kind, j, 16:32, :] = wide[:, share * j : share * j + 128].astype(BF16)

        def send(peer, place):
            pltpu.make_async_remote_copy(
                src_ref=sbuf.at[box, kind, place],
                dst_ref=rbuf.at[c, kind, d],
                send_sem=x_send.at[box, kind],
                recv_sem=x_recv.at[c, kind],
                device_id={"pipe": other, "dp": peer} if for_other else {"dp": peer},
                device_id_type=MESH,
            ).start()

        each_peer(send, 1 if for_other else 0)
        if not for_other:
            rbuf[c, kind, d] = sbuf[c, kind, block]

    def all_here(c, kind):
        def these(number):
            many(rbuf.at[c, kind, pl.ds(0, number)], x_recv.at[c, kind]).wait()

        if kind == 0:
            these(n_dp - 1)
        else:

            @pl.when(spared & (c == c1))
            def _():
                these(n_dp)

            @pl.when(jnp.logical_not(spared & (c == c1)))
            def _():
                these(n_dp - 1)

    def many(ref, sem):
        return pltpu.make_async_copy(ref, ref, sem)

    def project(x2, j, weights, w, sums):
        low, high = sums
        low = low + mm(x2, weights[w, piece * j : piece * (j + 1), :])
        high = high + mm(x2, weights[w, half + piece * j : half + piece * (j + 1), :])
        return low, high

    def branch(parts, j):
        low = high = 0.0
        for narrow, weights, w in parts:
            low = low + mm(narrow, weights[w, :, piece * j : piece * (j + 1)])
            high = high + mm(narrow, weights[w, :, half + piece * j : half + piece * (j + 1)])
        return jnp.concatenate([low[:8], high[8:]], axis=0)

    def add_branch(out, x, parts, sent=None):
        for j in pieces:
            at = piece_at(j)
            out[:, at] = (x[:, at].astype(F32) + branch(parts, j)).astype(BF16)
            if sent is not None:
                sent(j)

    def activate(pre, w):
        logistic = 0.5 + 0.5 * jnp.tanh(0.5 * pre)
        slopes[w] = logistic * (1.0 + pre * (1.0 - logistic))
        return pre * logistic

    def nothing():
        zeros = jnp.zeros((16, w_in.shape[2]), F32)
        return zeros, zeros

    def gather(sums):
        return sums[0][:8] + sums[1][8:]

    def forward_one(n):
        sums = nothing()
        for j in pieces:
            sums = project(xs[0, n, :, piece_at(j)], j, w_in, c1, sums)
        act = activate(gather(sums), c1)
        small[0, n] = act
        return [(twice(act), w_out, c1)]

    def forward_pair(ph, arrived, sent):
        a, b = pairs[ph]
        sums_a, sums_b = nothing(), nothing()
        for j in pieces:
            arrived(j)
            x2 = xs[ph, 0, :, piece_at(j)]
            sums_a = project(x2, j, w_in, a, sums_a)
            sums_b = project(x2, j, w_in, b, sums_b)
        act_a = activate(gather(sums_a), a)
        small[ph, 0] = act_a
        act_a = twice(act_a)
        act_b = activate(gather(sums_b) + mm(act_a, m_fwd[ph])[:8], b)
        small[ph, 1] = act_b
        parts = [(act_a, w_out, a), (twice(act_b), w_out, b)]
        add_branch(give.at[ph], xs.at[ph, 0], parts, sent)

    def backward_pair(ph, arrived):
        a, b = pairs[3 - ph]
        sums_a, sums_b = nothing(), nothing()
        for j in pieces:
            arrived(j)
            g2 = xs[ph, 0, :, piece_at(j)]
            sums_b = project(g2, j, t_out, b, sums_b)
            sums_a = project(g2, j, t_out, a, sums_a)
        grad_b = gather(sums_b) * slopes[b]
        small[ph, 0] = grad_b
        grad_b = twice(grad_b)
        grad_a = (gather(sums_a) + mm(grad_b, m_bwd[3 - ph])[:8]) * slopes[a]
        small[ph, 1] = grad_a
        return [(grad_b, t_in, b), (twice(grad_a), t_in, a)]

    def between(blk):
        a, b = pairs[blk]
        both = mm(w_out[a], w_in[b])
        m_fwd[blk] = both.astype(BF16)
        m_bwd[blk] = both.T.astype(BF16)

    def turn():
        tile = w_in.shape[2]

        def one(n, carry):
            w, at = n // (2 * half // tile), n % (2 * half // tile)
            at = pl.ds(pl.multiple_of(at * tile, tile), tile)
            t_in[w, :, at] = w_in[w, at, :].T
            t_out[w, at, :] = w_out[w, :, at].T
            return carry

        lax.fori_loop(0, 4 * (2 * half // tile), one, 0)

    def unpack(c, kind):
        all_here(c, kind)
        rows = rbuf[c, kind].astype(F32)
        flat = lambda part: part.reshape(n_dp * 8, 128)
        narrow = jnp.concatenate([flat(rows[:, 0:8]), flat(rows[:, 8:16])], axis=1)
        broad = jnp.where(path == 0, flat(rows[:, 16:24]), flat(rows[:, 24:32]))
        return narrow.astype(BF16), broad

    def prepare():
        for c in (0, 1):
            act, x = unpack(c, 0)
            act_rows[c] = act
            x_turned[c] = x.T.astype(BF16)

    def finish(c):
        grad_pre, grad_y = unpack(c, 1)
        gin_ref[0, c] = mm(x_turned[c], grad_pre)[:share]
        gout_ref[0, c] = mm(grad_y.T.astype(BF16), act_rows[c])[:share]

    early = 1 - chip // (chips // 2)

    def seeds():
        all_rows.wait()
        mine = lax.broadcasted_iota(jnp.int32, (16, 128), 0) + 8 * block
        every = lax.broadcasted_iota(jnp.int32, (128, 128), 0)

        def count(group, total):
            left, right = [], []
            for n in range(8):
                tile = ids_all[group * 8 + n]
                events = jnp.where(path == 0, tile[0:1, :], tile[1:2, :])
                left.append(jnp.where(mine == events, 1.0, 0.0).astype(BF16))
                right.append(jnp.where(every == tile[2:3, :], 1.0, 0.0).astype(BF16))
            return total + mm_t(jnp.concatenate(left, axis=1), jnp.concatenate(right, axis=1))

        counts = lax.fori_loop(0, n_dp // 8, count, jnp.zeros((16, 128), F32))[:8]
        sixteens = jnp.floor(counts * 0.0625)
        parts = jnp.concatenate([sixteens, counts - 16.0 * sixteens], axis=0).astype(BF16)
        sums = mm(parts, cand_ref[...])
        xs[2, 0] = fold((16.0 * sums[:8] + sums[8:]) * scale).astype(BF16)

    @pl.when(starts & (k == 0))
    def _():
        own_rows.wait()
        rows = first_rows[...].astype(F32)
        mine = jnp.where(block % 2 == 0, rows[:8], rows[8:])
        xs[0, 0] = fold(mine).astype(BF16)
        for copy in load(c1):
            copy.wait()
        add_branch(xs.at[0, 1], xs.at[0, 0], forward_one(0))

    @pl.when(relay & (k > 0) & (k < last))
    def _():
        pl.semaphore_wait(barrier, n_dp + 2)

    @pl.when(relay & edge)
    def _():
        pl.semaphore_wait(barrier, n_dp + 1)

    @pl.when(jnp.logical_not(relay))
    def _():
        pl.semaphore_wait(barrier, n_dp)

    @pl.when(k == 0)
    def _():
        @pl.when(starts)
        def _():
            pass_on().start()

        @pl.when(jnp.logical_not(starts))
        def _():
            for copy in load(c1):
                copy.wait()
            pass_on().wait_recv()
            add_branch(
                give.at[0], xs.at[0, 1], forward_one(1), lambda j: hop(0, j, up).start()
            )

    @pl.when(jnp.logical_not(relay))
    def _():
        @pl.when(k == 0)
        def _():
            back().start()

        for copy in lend(c1):
            copy.start()
        for copy in lend(c1):
            copy.wait_send()
        for copy in lend(c2):
            copy.start()

        @pl.when(k > 0)
        def _():
            for copy in mail(0):
                copy.wait_recv()

        spread(0, 1 - own(0))
        for ph in (1, 2):
            for copy in mail(ph):
                copy.wait_recv()
            spread(ph, 1 - own(ph))
        prepare()

        @pl.when(k == 0)
        def _():
            finish(early)

        @pl.when(k > 0)
        def _():
            for copy in mail(3):
                copy.wait_recv()
            spread(3, 1 - own(3))
            finish(early)

        finish(1 - early)
        for copy in lend(c2):
            copy.wait_send()

        @pl.when(k == 0)
        def _():
            back().wait_send()

    @pl.when(relay)
    def _():
        def from_below(ph):
            def wait(j):
                @pl.when(k > 0)
                def _():
                    hop(ph, j, down).wait_recv()

            return wait

        def from_above(ph):
            def wait(j):
                @pl.when(k < last)
                def _():
                    hop(ph, j, up).wait_recv()

            return wait

        def to_above(ph):
            def send(j):
                @pl.when(k < last)
                def _():
                    hop(ph, j, up).start()

            return send

        def to_below(ph):
            def send(j):
                @pl.when(k > 0)
                def _():
                    hop(ph, j, down).start()

            return send

        def lent(blk):
            for copy in lend((c1, c2)[blk]):
                copy.wait_recv()

        def middle(ph):
            w = pairs[ph][0] if ph < 2 else pairs[3 - ph][1]
            weights = w_out if ph < 2 else t_in
            add_branch(xs.at[ph, 1], xs.at[ph, 0], [(twice(small[ph, 0]), weights, w)])

        def post(ph):
            for copy in mail(ph):
                copy.start()

        def settle(ph):
            middle(ph)
            post(ph)
            spread(ph, own(ph))

        @pl.when(k == 0)
        def _():
            spread_ids()
            spread(0, own(0))
            lent(0)
            between(0)
            for copy in load(c2):
                copy.wait()
            lent(1)
            between(1)
            turn()
            many(ids_all.at[pl.ds(0, n_dp - 1)], ids_recv).wait()
            seeds()
            back().wait_recv()

        @pl.when(k > 0)
        def _():
            for copy in load(c1):
                copy.wait()
            lent(0)
            between(0)

            @pl.when(k == last)
            def _():
                spread_ids()
                for copy in load(c2):
                    copy.wait()
                lent(1)
                between(1)

            forward_pair(0, from_below(0), to_above(0))

            @pl.when(k == last)
            def _():
                xs[1, 0] = give[0]

            @pl.when(k < last)
            def _():
                settle(0)
                for copy in load(c2):
                    copy.wait()
                lent(1)
                between(1)

                @pl.when(k < chips // 2)
                def _():
                    turn()

        forward_pair(1, from_above(1), to_below(1))

        @pl.when(k > 0)
        def _():
            settle(1)

            @pl.when(k == last)
            def _():
                settle(0)

            @pl.when(k >= chips // 2)
            def _():
                turn()

        parts = backward_pair(2, from_below(2))
        add_branch(give.at[2], xs.at[2, 0], parts, to_above(2))

        @pl.when(k < last)
        def _():
            @pl.when(k == 0)
            def _():
                settle(1)

            settle(2)
            prepare()

            @pl.when(k == 0)
            def _():
                finish(early)

        @pl.when(k == last)
        def _():
            xs[3, 0] = give[2]

        parts = backward_pair(3, from_above(3))

        @pl.when(k > 0)
        def _():
            add_branch(give.at[3], xs.at[3, 0], parts, to_below(3))
            settle(3)

        @pl.when(k == 0)
        def _():
            @pl.when(path == 0)
            def _():
                spread(3, 0)
                middle(3)
                spread(3, 1, True)

            @pl.when(path == 1)
            def _():
                spread(3, 0, True)
                middle(3)
                spread(3, 1)

        @pl.when(k == last)
        def _():
            settle(2)
            prepare()

        @pl.when(k > 0)
        def _():
            finish(early)

        finish(1 - early)

        @pl.when(k < last)
        def _():
            for j in pieces:
                hop(2, j, up).wait_send()

        @pl.when((k > 0) & (k < last))
        def _():
            for j in pieces:
                hop(0, j, up).wait_send()

        @pl.when(k > 0)
        def _():
            for j in pieces:
                hop(1, j, down).wait_send()
                hop(3, j, down).wait_send()
            for ph in (0, 3):
                for copy in mail(ph):
                    copy.wait_send()

        for ph in (1, 2):
            for copy in mail(ph):
                copy.wait_send()

        @pl.when(k == 0)
        def _():
            many(rbuf.at[0, 0], x_send.at[2, 1]).wait()

        @pl.when(k == last)
        def _():
            many(ids_all.at[pl.ds(0, n_dp - 1)], ids_recv).wait()

        @pl.when(edge)
        def _():
            many(ids_all.at[pl.ds(0, n_dp - 1)], ids_send).wait()

    @pl.when(k == 0)
    def _():
        @pl.when(starts)
        def _():
            pass_on().wait_send()

        @pl.when(jnp.logical_not(starts))
        def _():
            for j in pieces:
                hop(0, j, up).wait_send()

    def gone(c, kind):
        many(rbuf.at[c, kind, pl.ds(0, n_dp - 1)], x_send.at[c, kind]).wait()

    for ph in range(3):
        gone(cs[ph], ph // 2)

    @pl.when(jnp.logical_not(spared))
    def _():
        gone(cs[3], 1)


def local(n_pipe, n_dp, item_ids, plan_order, candidates, adapters_in, adapters_out):
    batches, width = item_ids.shape
    events = width - 1
    _, _, features, hidden = adapters_in.shape
    share = features // n_dp
    scale = 1.0 / math.sqrt(batches * n_dp * events)
    ids = item_ids + candidates.shape[0] * plan_order[:, None]
    vmem = pl.BlockSpec(memory_space=pltpu.VMEM)
    hbm = pl.BlockSpec(memory_space=pltpu.HBM)
    grad_in, grad_out = pl.pallas_call(
        functools.partial(kernel, n_pipe, n_dp, scale),
        out_shape=(
            jax.ShapeDtypeStruct((1, 2, share, hidden), F32),
            jax.ShapeDtypeStruct((1, 2, share, hidden), F32),
        ),
        in_specs=[hbm] * 4,
        out_specs=(vmem, vmem),
        scratch_shapes=[
            pltpu.VMEM((4, features, hidden), BF16),
            pltpu.VMEM((4, hidden, features), BF16),
            pltpu.VMEM((4, hidden, features), BF16),
            pltpu.VMEM((4, features, hidden), BF16),
            pltpu.VMEM((2, hidden, hidden), BF16),
            pltpu.VMEM((2, hidden, hidden), BF16),
            pltpu.VMEM(ids.shape, jnp.int32),
            pltpu.VMEM(candidates.shape, BF16),
            pltpu.VMEM((16, features), BF16),
            pltpu.VMEM((8, 128), jnp.int32),
            pltpu.VMEM((n_dp, 8, 128), jnp.int32),
            pltpu.VMEM((4, 2, 16, features // 2), BF16),
            pltpu.VMEM((4, 16, features // 2), BF16),
            pltpu.VMEM((4, 2, 8, hidden), F32),
            pltpu.VMEM((4, 8, hidden), F32),
            pltpu.VMEM((3, 2, n_dp // 2, 32, 128), BF16),
            pltpu.VMEM((2, 2, n_dp, 32, 128), BF16),
            pltpu.VMEM((2, 128, n_dp * 8), BF16),
            pltpu.VMEM((2, n_dp * 8, hidden), BF16),
            pltpu.SemaphoreType.DMA((2, 2)),
            pltpu.SemaphoreType.DMA((3,)),
            pltpu.SemaphoreType.DMA((2, 2)),
            pltpu.SemaphoreType.DMA((2, 2)),
            pltpu.SemaphoreType.DMA((4, PIECES)),
            pltpu.SemaphoreType.DMA((4, PIECES)),
            pltpu.SemaphoreType.DMA((4, 2)),
            pltpu.SemaphoreType.DMA((4, 2)),
            pltpu.SemaphoreType.DMA,
            pltpu.SemaphoreType.DMA,
            pltpu.SemaphoreType.DMA,
            pltpu.SemaphoreType.DMA,
            pltpu.SemaphoreType.DMA,
            pltpu.SemaphoreType.DMA,
            pltpu.SemaphoreType.DMA((3, 2)),
            pltpu.SemaphoreType.DMA((2, 2)),
        ],
        compiler_params=pltpu.CompilerParams(
            collective_id=0, has_side_effects=True, vmem_limit_bytes=107 * 512 * 1024
        ),
    )(ids, candidates, adapters_in, adapters_out)
    return grad_in, jnp.swapaxes(grad_out, 2, 3)


def solution(mesh):
    in_specs = (P(None, "dp"), P(), P(), P("pipe", None, None, None), P("pipe", None, None, None))
    out_specs = (P("pipe", None, "dp", None), P("pipe", None, None, "dp"))
    return jax.shard_map(
        functools.partial(local, mesh.shape["pipe"], mesh.shape["dp"]),
        mesh=mesh,
        in_specs=in_specs,
        out_specs=out_specs,
        check_vma=False,
    )
```

```python
import functools
import math

import jax
import jax.numpy as jnp
from jax import lax
from jax.experimental import pallas as pl
from jax.experimental.pallas import tpu as pltpu
from jax.sharding import PartitionSpec as P

MESH = pl.DeviceIdType.MESH
F32 = jnp.float32
BF16 = jnp.bfloat16
PIECES = 3


def mm(a, b):
    return jnp.dot(a, b, preferred_element_type=F32)


def mm_t(a, b):
    return lax.dot_general(a, b, (((1,), (1,)), ((), ())), preferred_element_type=F32)


def t_mm(a, b):
    return lax.dot_general(a, b, (((0,), (0,)), ((), ())), preferred_element_type=F32)


def fold(wide):
    half = wide.shape[1] // 2
    return jnp.concatenate([wide[:, :half], wide[:, half:]], axis=0)


def twice(rows):
    return jnp.concatenate([rows, rows], axis=0).astype(BF16)


def kernel(
    n_pipe,
    n_dp,
    scale,
    ids_hbm,
    cand_hbm,
    win_ref,
    wout_ref,
    gin_ref,
    gout_ref,
    w_in,
    w_out,
    t_in,
    t_out,
    m_fwd,
    m_bwd,
    ids_ref,
    cand_ref,
    first_rows,
    ids_own,
    ids_all,
    xs,
    give,
    small,
    slopes,
    sbuf,
    rbuf,
    x_turned,
    act_rows,
    w_sem,
    cand_sem,
    share_send,
    share_recv,
    give_sem,
    got_sem,
    mail_send,
    mail_recv,
    pass_send,
    pass_recv,
    back_send,
    back_recv,
    ids_send,
    ids_recv,
    x_send,
    x_recv,
    met,
):
    p = lax.axis_index("pipe")
    d = lax.axis_index("dp")
    half_dp = n_dp // 2
    path = d // half_dp
    block = d % half_dp
    c1 = path
    c2 = 1 - path
    chips = n_pipe // 2
    chip = p // 2
    core = p % 2
    relay = core == 1
    starts = core == path
    other = p + 1 - 2 * core
    last = chips - 1
    k = chip + path * (last - 2 * chip)
    up = 2 * chip + 3 - 4 * path
    down = 2 * chip - 1 + 4 * path
    edge = (k == 0) | (k == last)
    half = w_in.shape[1] // 2
    n_items = cand_ref.shape[0]
    piece = half // PIECES
    pieces = range(PIECES)
    pairs = ((c1 + 2 - 2 * path, c1 + 2 * path), (c2 + 2 * path, c2 + 2 - 2 * path))

    spared = (core == 0) & (k == 0)

    def own(ph):
        return (ph + 1 + path) % 2

    share = 2 * half // n_dp
    cs = (c1, c2, c2, c1)

    def load(c):
        return (
            pltpu.make_async_copy(win_ref.at[0, c], w_in.at[c], w_sem.at[c, 0]),
            pltpu.make_async_copy(wout_ref.at[0, c], w_out.at[c], w_sem.at[c, 1]),
        )

    def lend(c):
        return [
            pltpu.make_async_remote_copy(
                src_ref=src.at[0, c],
                dst_ref=dst.at[2 + c],
                send_sem=share_send.at[c, n],
                recv_sem=share_recv.at[c, n],
                device_id={"pipe": other},
                device_id_type=MESH,
            )
            for n, (src, dst) in enumerate(((win_ref, w_in), (wout_ref, w_out)))
        ]

    start = pl.multiple_of(16 * (block // 2), 16)
    own_rows = pltpu.make_async_copy(cand_hbm.at[pl.ds(start, 16)], first_rows, cand_sem.at[0])
    all_rows = pltpu.make_async_copy(cand_hbm, cand_ref, cand_sem.at[1])

    id_copy = pltpu.make_async_copy(ids_hbm, ids_ref, cand_sem.at[2])

    @pl.when(starts & (k == 0))
    def _():
        own_rows.start()

    @pl.when(relay | (k == 0))
    def _():
        for copy in load(c1):
            copy.start()

    @pl.when(relay)
    def _():
        @pl.when(edge)
        def _():
            id_copy.start()

        for copy in load(c2):
            copy.start()

        @pl.when(k == 0)
        def _():
            all_rows.start()

    side, row, column = d // 16, (d // 4) % 4, d % 4
    planes = [16 * ((side + 1) % 2), 16 * side]
    columns = [(column + away) % 4 for away in (2, 1, 3, 0)]

    def each_peer(do, too=0):
        def line(n, carry):
            at = 4 * ((row + (2 + 3 * (n * (n + 1) // 2)) % 4) % 4)
            for x in columns:
                for z in planes:
                    do(z + at + x, at + x)
            return carry

        lax.fori_loop(0, 3, line, 0)
        near = [(z, x) for x in columns for z in planes]
        for z, x in near[: 7 + too]:
            do(z + 4 * row + x, 4 * row + x)

    barrier = pltpu.get_barrier_semaphore()

    def hello(to):
        pl.semaphore_signal(barrier, inc=1, device_id={"pipe": to}, device_id_type=MESH)

    hello(other)

    @pl.when(relay & (k < last))
    def _():
        hello(up)

    @pl.when(relay & (k > 0))
    def _():
        hello(down)

    beside = [16 * side + 4 * row + (column + step) % 4 for step in (1, 3)]
    above = [16 * side + 4 * ((row + step) % 4) + column for step in (1, 3)]
    facing = 16 * ((side + 1) % 2) + 4 * row + column

    @pl.when(relay)
    def _():
        for peer in (*beside, *above, facing):
            pl.semaphore_signal(barrier, inc=1, device_id={"dp": peer}, device_id_type=MESH)

    def meet(n, peers):
        for peer in peers:
            pl.semaphore_signal(met.at[n], inc=1, device_id={"dp": peer}, device_id_type=MESH)

    def meet_own_plane():
        for n, peers in enumerate((beside, beside, above, above)):
            meet(n, peers)
            pl.semaphore_wait(met.at[n], 2)
        meet(4, [facing])

    def meet_other_plane():
        pl.semaphore_wait(met.at[4], 1)
        pl.semaphore_signal(met.at[5], inc=1, device_id={"pipe": other}, device_id_type=MESH)

    def piece_at(j):
        return pl.ds(j * piece, piece)

    def hop(ph, j, to):
        return pltpu.make_async_remote_copy(
            src_ref=give.at[ph, :, piece_at(j)],
            dst_ref=xs.at[ph, 0, :, piece_at(j)],
            send_sem=give_sem.at[ph, j],
            recv_sem=got_sem.at[ph, j],
            device_id={"pipe": to},
            device_id_type=MESH,
        )

    def back():
        return pltpu.make_async_remote_copy(
            src_ref=slopes.at[c1],
            dst_ref=slopes.at[2 + c1],
            send_sem=back_send,
            recv_sem=back_recv,
            device_id={"pipe": other},
            device_id_type=MESH,
        )

    def pass_on():
        return pltpu.make_async_remote_copy(
            src_ref=xs.at[0, 1],
            dst_ref=xs.at[0, 1],
            send_sem=pass_send,
            recv_sem=pass_recv,
            device_id={"pipe": other},
            device_id_type=MESH,
        )

    def mail(ph):
        n = 1 - own(ph)
        return [
            pltpu.make_async_remote_copy(
                src_ref=ref.at[ph, n],
                dst_ref=ref.at[ph, n],
                send_sem=mail_send.at[ph, m],
                recv_sem=mail_recv.at[ph, m],
                device_id={"pipe": other},
                device_id_type=MESH,
            )
            for m, ref in enumerate((xs, small))
        ]

    def spread_ids():
        id_copy.wait()
        lane = lax.broadcasted_iota(jnp.int32, (1, 128), 1)
        front = back = target = jnp.full((1, 128), -1, jnp.int32)
        ids_own[...] = jnp.full((8, 128), -1, jnp.int32)
        ids_own[0:4, 0:33] = ids_ref[...]
        for m in range(4):
            row = ids_own[m : m + 1, :]
            is_front = row < 2 * n_items
            for above in (2 * n_items, n_items):
                row = jnp.where(row >= above, row - above, row)
            fronts = jnp.where(is_front, row, -1)
            backs = jnp.where(is_front, -1, row)
            here = lane // 32 == m
            front = jnp.where(here, pltpu.roll(fronts, 32 * m, 1) if m else fronts, front)
            back = jnp.where(here, pltpu.roll(backs, 32 * m, 1) if m else backs, back)
            target = jnp.where(here, pltpu.roll(row, (32 * m + 127) % 128, 1), target)
        ids_own[0:1, :] = front
        ids_own[1:2, :] = back
        ids_own[2:3, :] = target
        ids_all[d] = ids_own[...]

        def send(peer, place):
            pltpu.make_async_remote_copy(
                src_ref=ids_own,
                dst_ref=ids_all.at[d],
                send_sem=ids_send,
                recv_sem=ids_recv,
                device_id={"dp": peer},
                device_id_type=MESH,
            ).start()

        each_peer(send)

    def spread(ph, n, for_other=False):
        c, kind = cs[ph], ph // 2
        box = 2 if for_other else c
        narrow, broad = small.at[ph, n], xs.at[ph, n]
        narrow, broad = narrow[...], broad[...].astype(F32)
        hidden = narrow.shape[1] // 2
        top = jnp.concatenate([narrow[:, :hidden], narrow[:, hidden:]], axis=0).astype(BF16)
        wide = jnp.concatenate([broad, broad[:, :128]], axis=1)
        for j in range(half_dp):
            sbuf[box, kind, j, 0:16, :] = top
            sbuf[box, kind, j, 16:32, :] = wide[:, share * j : share * j + 128].astype(BF16)

        def send(peer, place):
            pltpu.make_async_remote_copy(
                src_ref=sbuf.at[box, kind, place],
                dst_ref=rbuf.at[c, kind, d],
                send_sem=x_send.at[box, kind],
                recv_sem=x_recv.at[c, kind],
                device_id={"pipe": other, "dp": peer} if for_other else {"dp": peer},
                device_id_type=MESH,
            ).start()

        each_peer(send, 1 if for_other else 0)
        if not for_other:
            rbuf[c, kind, d] = sbuf[c, kind, block]

    def all_here(c, kind):
        def these(number):
            many(rbuf.at[c, kind, pl.ds(0, number)], x_recv.at[c, kind]).wait()

        if kind == 0:
            these(n_dp - 1)
        else:

            @pl.when(spared & (c == c1))
            def _():
                these(n_dp)

            @pl.when(jnp.logical_not(spared & (c == c1)))
            def _():
                these(n_dp - 1)

    def many(ref, sem):
        return pltpu.make_async_copy(ref, ref, sem)

    def project(x2, j, weights, w, sums):
        low, high = sums
        low = low + mm(x2, weights[w, piece * j : piece * (j + 1), :])
        high = high + mm(x2, weights[w, half + piece * j : half + piece * (j + 1), :])
        return low, high

    def branch(parts, j):
        low = high = 0.0
        for narrow, weights, w in parts:
            low = low + mm(narrow, weights[w, :, piece * j : piece * (j + 1)])
            high = high + mm(narrow, weights[w, :, half + piece * j : half + piece * (j + 1)])
        return jnp.concatenate([low[:8], high[8:]], axis=0)

    def add_branch(out, x, parts, sent=None):
        for j in pieces:
            at = piece_at(j)
            out[:, at] = (x[:, at].astype(F32) + branch(parts, j)).astype(BF16)
            if sent is not None:
                sent(j)

    def activate(pre, w):
        logistic = 0.5 + 0.5 * jnp.tanh(0.5 * pre)
        slopes[w] = logistic * (1.0 + pre * (1.0 - logistic))
        return pre * logistic

    def nothing():
        zeros = jnp.zeros((16, w_in.shape[2]), F32)
        return zeros, zeros

    def gather(sums):
        return sums[0][:8] + sums[1][8:]

    def forward_one(n):
        sums = nothing()
        for j in pieces:
            sums = project(xs[0, n, :, piece_at(j)], j, w_in, c1, sums)
        act = activate(gather(sums), c1)
        small[0, n] = act
        return [(twice(act), w_out, c1)]

    def forward_pair(ph, arrived, sent):
        a, b = pairs[ph]
        sums_a, sums_b = nothing(), nothing()
        for j in pieces:
            arrived(j)
            x2 = xs[ph, 0, :, piece_at(j)]
            sums_a = project(x2, j, w_in, a, sums_a)
            sums_b = project(x2, j, w_in, b, sums_b)
        act_a = activate(gather(sums_a), a)
        small[ph, 0] = act_a
        act_a = twice(act_a)
        act_b = activate(gather(sums_b) + mm(act_a, m_fwd[ph])[:8], b)
        small[ph, 1] = act_b
        parts = [(act_a, w_out, a), (twice(act_b), w_out, b)]
        add_branch(give.at[ph], xs.at[ph, 0], parts, sent)

    def backward_pair(ph, arrived):
        a, b = pairs[3 - ph]
        sums_a, sums_b = nothing(), nothing()
        for j in pieces:
            arrived(j)
            g2 = xs[ph, 0, :, piece_at(j)]
            sums_b = project(g2, j, t_out, b, sums_b)
            sums_a = project(g2, j, t_out, a, sums_a)
        grad_b = gather(sums_b) * slopes[b]
        small[ph, 0] = grad_b
        grad_b = twice(grad_b)
        grad_a = (gather(sums_a) + mm(grad_b, m_bwd[3 - ph])[:8]) * slopes[a]
        small[ph, 1] = grad_a
        return [(grad_b, t_in, b), (twice(grad_a), t_in, a)]

    def between(blk):
        a, b = pairs[blk]
        both = mm(w_out[a], w_in[b])
        m_fwd[blk] = both.astype(BF16)
        m_bwd[blk] = both.T.astype(BF16)

    def turn():
        tile = w_in.shape[2]

        def one(n, carry):
            w, at = n // (2 * half // tile), n % (2 * half // tile)
            at = pl.ds(pl.multiple_of(at * tile, tile), tile)
            t_in[w, :, at] = w_in[w, at, :].T
            t_out[w, at, :] = w_out[w, :, at].T
            return carry

        lax.fori_loop(0, 4 * (2 * half // tile), one, 0)

    def unpack(c, kind):
        all_here(c, kind)
        rows = rbuf[c, kind].astype(F32)
        flat = lambda part: part.reshape(n_dp * 8, 128)
        narrow = jnp.concatenate([flat(rows[:, 0:8]), flat(rows[:, 8:16])], axis=1)
        broad = jnp.where(path == 0, flat(rows[:, 16:24]), flat(rows[:, 24:32]))
        return narrow.astype(BF16), broad

    def prepare():
        for c in (0, 1):
            act, x = unpack(c, 0)
            act_rows[c] = act
            x_turned[c] = x.T.astype(BF16)

    def finish(c):
        grad_pre, grad_y = unpack(c, 1)
        gin_ref[0, c] = mm(x_turned[c], grad_pre)[:share]
        gout_ref[0, c] = mm(grad_y.T.astype(BF16), act_rows[c])[:share]

    early = 1 - chip // (chips // 2)

    def seeds():
        all_rows.wait()
        mine = lax.broadcasted_iota(jnp.int32, (16, 128), 0) + 8 * block
        every = lax.broadcasted_iota(jnp.int32, (128, 128), 0)

        def count(group, total):
            left, right = [], []
            for n in range(8):
                tile = ids_all[group * 8 + n]
                events = jnp.where(path == 0, tile[0:1, :], tile[1:2, :])
                left.append(jnp.where(mine == events, 1.0, 0.0).astype(BF16))
                right.append(jnp.where(every == tile[2:3, :], 1.0, 0.0).astype(BF16))
            return total + mm_t(jnp.concatenate(left, axis=1), jnp.concatenate(right, axis=1))

        counts = lax.fori_loop(0, n_dp // 8, count, jnp.zeros((16, 128), F32))[:8]
        sixteens = jnp.floor(counts * 0.0625)
        parts = jnp.concatenate([sixteens, counts - 16.0 * sixteens], axis=0).astype(BF16)
        sums = mm(parts, cand_ref[...])
        xs[2, 0] = fold((16.0 * sums[:8] + sums[8:]) * scale).astype(BF16)

    @pl.when(starts & (k == 0))
    def _():
        own_rows.wait()
        rows = first_rows[...].astype(F32)
        mine = jnp.where(block % 2 == 0, rows[:8], rows[8:])
        xs[0, 0] = fold(mine).astype(BF16)
        for copy in load(c1):
            copy.wait()
        add_branch(xs.at[0, 1], xs.at[0, 0], forward_one(0))

    @pl.when(relay & (k > 0) & (k < last))
    def _():
        pl.semaphore_wait(barrier, 8)

    @pl.when(relay & edge)
    def _():
        pl.semaphore_wait(barrier, 7)

    @pl.when(jnp.logical_not(relay))
    def _():
        pl.semaphore_wait(barrier, 1)

    @pl.when(k == 0)
    def _():
        @pl.when(starts)
        def _():
            pass_on().start()

        @pl.when(jnp.logical_not(starts))
        def _():
            for copy in load(c1):
                copy.wait()
            pass_on().wait_recv()
            add_branch(
                give.at[0], xs.at[0, 1], forward_one(1), lambda j: hop(0, j, up).start()
            )

    @pl.when(jnp.logical_not(relay))
    def _():
        @pl.when(k == 0)
        def _():
            back().start()

        for copy in lend(c1):
            copy.start()
        for copy in lend(c1):
            copy.wait_send()
        for copy in lend(c2):
            copy.start()

        @pl.when(k > 0)
        def _():
            for copy in mail(0):
                copy.wait_recv()

        pl.semaphore_wait(met.at[5], 1)
        spread(0, 1 - own(0))
        for ph in (1, 2):
            for copy in mail(ph):
                copy.wait_recv()
            spread(ph, 1 - own(ph))
        prepare()

        @pl.when(k == 0)
        def _():
            finish(early)

        @pl.when(k > 0)
        def _():
            for copy in mail(3):
                copy.wait_recv()
            spread(3, 1 - own(3))
            finish(early)

        finish(1 - early)
        for copy in lend(c2):
            copy.wait_send()

        @pl.when(k == 0)
        def _():
            back().wait_send()

    @pl.when(relay)
    def _():
        def from_below(ph):
            def wait(j):
                @pl.when(k > 0)
                def _():
                    hop(ph, j, down).wait_recv()

            return wait

        def from_above(ph):
            def wait(j):
                @pl.when(k < last)
                def _():
                    hop(ph, j, up).wait_recv()

            return wait

        def to_above(ph):
            def send(j):
                @pl.when(k < last)
                def _():
                    hop(ph, j, up).start()

            return send

        def to_below(ph):
            def send(j):
                @pl.when(k > 0)
                def _():
                    hop(ph, j, down).start()

            return send

        def lent(blk):
            for copy in lend((c1, c2)[blk]):
                copy.wait_recv()

        def middle(ph):
            w = pairs[ph][0] if ph < 2 else pairs[3 - ph][1]
            weights = w_out if ph < 2 else t_in
            add_branch(xs.at[ph, 1], xs.at[ph, 0], [(twice(small[ph, 0]), weights, w)])

        def post(ph):
            for copy in mail(ph):
                copy.start()

        def settle(ph):
            middle(ph)
            post(ph)
            spread(ph, own(ph))

        @pl.when(k == 0)
        def _():
            meet_own_plane()
            meet_other_plane()
            spread_ids()
            spread(0, own(0))
            lent(0)
            between(0)
            for copy in load(c2):
                copy.wait()
            lent(1)
            between(1)
            turn()
            many(ids_all.at[pl.ds(0, n_dp - 1)], ids_recv).wait()
            seeds()
            back().wait_recv()

        @pl.when(k > 0)
        def _():
            @pl.when(k > 1)
            def _():
                meet_own_plane()

            for copy in load(c1):
                copy.wait()
            lent(0)
            between(0)

            @pl.when(k == last)
            def _():
                meet_other_plane()
                spread_ids()
                for copy in load(c2):
                    copy.wait()
                lent(1)
                between(1)

            forward_pair(0, from_below(0), to_above(0))

            @pl.when(k == last)
            def _():
                xs[1, 0] = give[0]

            @pl.when(k == 1)
            def _():
                meet_own_plane()

            @pl.when(k < last)
            def _():
                meet_other_plane()
                settle(0)
                for copy in load(c2):
                    copy.wait()
                lent(1)
                between(1)

                @pl.when(k < chips // 2)
                def _():
                    turn()

        forward_pair(1, from_above(1), to_below(1))

        @pl.when(k > 0)
        def _():
            settle(1)

            @pl.when(k == last)
            def _():
                settle(0)

            @pl.when(k >= chips // 2)
            def _():
                turn()

        parts = backward_pair(2, from_below(2))
        add_branch(give.at[2], xs.at[2, 0], parts, to_above(2))

        @pl.when(k < last)
        def _():
            @pl.when(k == 0)
            def _():
                settle(1)

            settle(2)
            prepare()

            @pl.when(k == 0)
            def _():
                finish(early)

        @pl.when(k == last)
        def _():
            xs[3, 0] = give[2]

        parts = backward_pair(3, from_above(3))

        @pl.when(k > 0)
        def _():
            add_branch(give.at[3], xs.at[3, 0], parts, to_below(3))
            settle(3)

        @pl.when(k == 0)
        def _():
            @pl.when(path == 0)
            def _():
                spread(3, 0)
                middle(3)
                spread(3, 1, True)

            @pl.when(path == 1)
            def _():
                spread(3, 0, True)
                middle(3)
                spread(3, 1)

        @pl.when(k == last)
        def _():
            settle(2)
            prepare()

        @pl.when(k > 0)
        def _():
            finish(early)

        finish(1 - early)

        @pl.when(k < last)
        def _():
            for j in pieces:
                hop(2, j, up).wait_send()

        @pl.when((k > 0) & (k < last))
        def _():
            for j in pieces:
                hop(0, j, up).wait_send()

        @pl.when(k > 0)
        def _():
            for j in pieces:
                hop(1, j, down).wait_send()
                hop(3, j, down).wait_send()
            for ph in (0, 3):
                for copy in mail(ph):
                    copy.wait_send()

        for ph in (1, 2):
            for copy in mail(ph):
                copy.wait_send()

        @pl.when(k == 0)
        def _():
            many(rbuf.at[0, 0], x_send.at[2, 1]).wait()

        @pl.when(k == last)
        def _():
            many(ids_all.at[pl.ds(0, n_dp - 1)], ids_recv).wait()

        @pl.when(edge)
        def _():
            many(ids_all.at[pl.ds(0, n_dp - 1)], ids_send).wait()

    @pl.when(k == 0)
    def _():
        @pl.when(starts)
        def _():
            pass_on().wait_send()

        @pl.when(jnp.logical_not(starts))
        def _():
            for j in pieces:
                hop(0, j, up).wait_send()

    def gone(c, kind):
        many(rbuf.at[c, kind, pl.ds(0, n_dp - 1)], x_send.at[c, kind]).wait()

    for ph in range(3):
        gone(cs[ph], ph // 2)

    @pl.when(jnp.logical_not(spared))
    def _():
        gone(cs[3], 1)


def local(n_pipe, n_dp, item_ids, plan_order, candidates, adapters_in, adapters_out):
    batches, width = item_ids.shape
    events = width - 1
    _, _, features, hidden = adapters_in.shape
    share = features // n_dp
    scale = 1.0 / math.sqrt(batches * n_dp * events)
    ids = item_ids + candidates.shape[0] * plan_order[:, None]
    vmem = pl.BlockSpec(memory_space=pltpu.VMEM)
    hbm = pl.BlockSpec(memory_space=pltpu.HBM)
    grad_in, grad_out = pl.pallas_call(
        functools.partial(kernel, n_pipe, n_dp, scale),
        out_shape=(
            jax.ShapeDtypeStruct((1, 2, share, hidden), F32),
            jax.ShapeDtypeStruct((1, 2, share, hidden), F32),
        ),
        in_specs=[hbm] * 4,
        out_specs=(vmem, vmem),
        scratch_shapes=[
            pltpu.VMEM((4, features, hidden), BF16),
            pltpu.VMEM((4, hidden, features), BF16),
            pltpu.VMEM((4, hidden, features), BF16),
            pltpu.VMEM((4, features, hidden), BF16),
            pltpu.VMEM((2, hidden, hidden), BF16),
            pltpu.VMEM((2, hidden, hidden), BF16),
            pltpu.VMEM(ids.shape, jnp.int32),
            pltpu.VMEM(candidates.shape, BF16),
            pltpu.VMEM((16, features), BF16),
            pltpu.VMEM((8, 128), jnp.int32),
            pltpu.VMEM((n_dp, 8, 128), jnp.int32),
            pltpu.VMEM((4, 2, 16, features // 2), BF16),
            pltpu.VMEM((4, 16, features // 2), BF16),
            pltpu.VMEM((4, 2, 8, hidden), F32),
            pltpu.VMEM((4, 8, hidden), F32),
            pltpu.VMEM((3, 2, n_dp // 2, 32, 128), BF16),
            pltpu.VMEM((2, 2, n_dp, 32, 128), BF16),
            pltpu.VMEM((2, 128, n_dp * 8), BF16),
            pltpu.VMEM((2, n_dp * 8, hidden), BF16),
            pltpu.SemaphoreType.DMA((2, 2)),
            pltpu.SemaphoreType.DMA((3,)),
            pltpu.SemaphoreType.DMA((2, 2)),
            pltpu.SemaphoreType.DMA((2, 2)),
            pltpu.SemaphoreType.DMA((4, PIECES)),
            pltpu.SemaphoreType.DMA((4, PIECES)),
            pltpu.SemaphoreType.DMA((4, 2)),
            pltpu.SemaphoreType.DMA((4, 2)),
            pltpu.SemaphoreType.DMA,
            pltpu.SemaphoreType.DMA,
            pltpu.SemaphoreType.DMA,
            pltpu.SemaphoreType.DMA,
            pltpu.SemaphoreType.DMA,
            pltpu.SemaphoreType.DMA,
            pltpu.SemaphoreType.DMA((3, 2)),
            pltpu.SemaphoreType.DMA((2, 2)),
            pltpu.SemaphoreType.REGULAR((6,)),
        ],
        compiler_params=pltpu.CompilerParams(
            collective_id=0, has_side_effects=True, vmem_limit_bytes=107 * 512 * 1024
        ),
    )(ids, candidates, adapters_in, adapters_out)
    return grad_in, jnp.swapaxes(grad_out, 2, 3)


def solution(mesh):
    in_specs = (P(None, "dp"), P(), P(), P("pipe", None, None, None), P("pipe", None, None, None))
    out_specs = (P("pipe", None, "dp", None), P("pipe", None, None, "dp"))
    return jax.shard_map(
        functools.partial(local, mesh.shape["pipe"], mesh.shape["dp"]),
        mesh=mesh,
        in_specs=in_specs,
        out_specs=out_specs,
        check_vma=False,
    )
```

```python
import functools
import math

import jax
import jax.numpy as jnp
from jax import lax
from jax.experimental import pallas as pl
from jax.experimental.pallas import tpu as pltpu
from jax.sharding import PartitionSpec as P

MESH = pl.DeviceIdType.MESH
F32 = jnp.float32
BF16 = jnp.bfloat16
PIECES = 3


def mm(a, b):
    return jnp.dot(a, b, preferred_element_type=F32)


def mm_t(a, b):
    return lax.dot_general(a, b, (((1,), (1,)), ((), ())), preferred_element_type=F32)


def t_mm(a, b):
    return lax.dot_general(a, b, (((0,), (0,)), ((), ())), preferred_element_type=F32)


def fold(wide):
    half = wide.shape[1] // 2
    return jnp.concatenate([wide[:, :half], wide[:, half:]], axis=0)


def twice(rows):
    return jnp.concatenate([rows, rows], axis=0).astype(BF16)


def kernel(
    n_pipe,
    n_dp,
    scale,
    ids_hbm,
    cand_hbm,
    win_ref,
    wout_ref,
    gin_ref,
    gout_ref,
    w_in,
    w_out,
    t_in,
    t_out,
    m_fwd,
    m_bwd,
    ids_ref,
    cand_ref,
    first_rows,
    ids_own,
    ids_all,
    xs,
    give,
    small,
    slopes,
    bases,
    sbuf,
    rbuf,
    x_turned,
    act_rows,
    w_sem,
    cand_sem,
    share_send,
    share_recv,
    give_sem,
    got_sem,
    mail_send,
    mail_recv,
    pass_send,
    pass_recv,
    back_send,
    back_recv,
    ids_send,
    ids_recv,
    x_send,
    x_recv,
    met,
):
    p = lax.axis_index("pipe")
    d = lax.axis_index("dp")
    half_dp = n_dp // 2
    path = d // half_dp
    block = d % half_dp
    c1 = path
    c2 = 1 - path
    chips = n_pipe // 2
    chip = p // 2
    core = p % 2
    relay = core == 1
    starts = core == path
    other = p + 1 - 2 * core
    last = chips - 1
    k = chip + path * (last - 2 * chip)
    up = 2 * chip + 3 - 4 * path
    down = 2 * chip - 1 + 4 * path
    edge = (k == 0) | (k == last)
    half = w_in.shape[1] // 2
    n_items = cand_ref.shape[0]
    piece = half // PIECES
    pieces = range(PIECES)
    pairs = ((c1 + 2 - 2 * path, c1 + 2 * path), (c2 + 2 * path, c2 + 2 - 2 * path))

    spared = (core == 0) & (k == 0)

    def own(ph):
        return (ph + 1 + path) % 2

    share = 2 * half // n_dp
    cs = (c1, c2, c2, c1)

    def load(c):
        return (
            pltpu.make_async_copy(win_ref.at[0, c], w_in.at[c], w_sem.at[c, 0]),
            pltpu.make_async_copy(wout_ref.at[0, c], w_out.at[c], w_sem.at[c, 1]),
        )

    def lend(c):
        return [
            pltpu.make_async_remote_copy(
                src_ref=src.at[0, c],
                dst_ref=dst.at[2 + c],
                send_sem=share_send.at[c, n],
                recv_sem=share_recv.at[c, n],
                device_id={"pipe": other},
                device_id_type=MESH,
            )
            for n, (src, dst) in enumerate(((win_ref, w_in), (wout_ref, w_out)))
        ]

    start = pl.multiple_of(16 * (block // 2), 16)
    own_rows = pltpu.make_async_copy(cand_hbm.at[pl.ds(start, 16)], first_rows, cand_sem.at[0])
    all_rows = pltpu.make_async_copy(cand_hbm, cand_ref, cand_sem.at[1])

    id_copy = pltpu.make_async_copy(ids_hbm, ids_ref, cand_sem.at[2])

    @pl.when(starts & (k == 0))
    def _():
        own_rows.start()

    @pl.when(relay | (k == 0))
    def _():
        for copy in load(c1):
            copy.start()

    @pl.when(relay)
    def _():
        @pl.when(edge)
        def _():
            id_copy.start()

        for copy in load(c2):
            copy.start()

        @pl.when(k == 0)
        def _():
            all_rows.start()

    side, row, column = d // 16, (d // 4) % 4, d % 4
    planes = [16 * ((side + 1) % 2), 16 * side]
    columns = [(column + away) % 4 for away in (2, 1, 3, 0)]

    def each_peer(do, too=0):
        def line(n, carry):
            at = 4 * ((row + (2 + 3 * (n * (n + 1) // 2)) % 4) % 4)
            for x in columns:
                for z in planes:
                    do(z + at + x, at + x)
            return carry

        lax.fori_loop(0, 3, line, 0)
        near = [(z, x) for x in columns for z in planes]
        for z, x in near[: 7 + too]:
            do(z + 4 * row + x, 4 * row + x)

    barrier = pltpu.get_barrier_semaphore()

    def hello(to):
        pl.semaphore_signal(barrier, inc=1, device_id={"pipe": to}, device_id_type=MESH)

    hello(other)

    @pl.when(relay & (k < last))
    def _():
        hello(up)

    @pl.when(relay & (k > 0))
    def _():
        hello(down)

    beside = [16 * side + 4 * row + (column + step) % 4 for step in (1, 3)]
    above = [16 * side + 4 * ((row + step) % 4) + column for step in (1, 3)]
    facing = 16 * ((side + 1) % 2) + 4 * row + column

    @pl.when(relay)
    def _():
        for peer in (*beside, *above, facing):
            pl.semaphore_signal(barrier, inc=1, device_id={"dp": peer}, device_id_type=MESH)

    def meet(n, peers):
        for peer in peers:
            pl.semaphore_signal(met.at[n], inc=1, device_id={"dp": peer}, device_id_type=MESH)

    rounds = (beside, beside, above, above, [facing])

    def met_by(n):
        pl.semaphore_wait(met.at[n], 2)
        meet(n + 1, rounds[n + 1])

    def meet_other_plane():
        pl.semaphore_wait(met.at[4], 1)
        pl.semaphore_signal(met.at[5], inc=1, device_id={"pipe": other}, device_id_type=MESH)

    def piece_at(j):
        return pl.ds(j * piece, piece)

    def hop(ph, j, to):
        return pltpu.make_async_remote_copy(
            src_ref=give.at[ph, :, piece_at(j)],
            dst_ref=xs.at[ph, 0, :, piece_at(j)],
            send_sem=give_sem.at[ph, j],
            recv_sem=got_sem.at[ph, j],
            device_id={"pipe": to},
            device_id_type=MESH,
        )

    def back():
        return pltpu.make_async_remote_copy(
            src_ref=slopes.at[c1],
            dst_ref=slopes.at[2 + c1],
            send_sem=back_send,
            recv_sem=back_recv,
            device_id={"pipe": other},
            device_id_type=MESH,
        )

    def pass_on():
        return pltpu.make_async_remote_copy(
            src_ref=xs.at[0, 1],
            dst_ref=xs.at[0, 1],
            send_sem=pass_send,
            recv_sem=pass_recv,
            device_id={"pipe": other},
            device_id_type=MESH,
        )

    def mail(ph):
        n = 1 - own(ph)
        return [
            pltpu.make_async_remote_copy(
                src_ref=ref.at[ph, n],
                dst_ref=ref.at[ph, n],
                send_sem=mail_send.at[ph, m],
                recv_sem=mail_recv.at[ph, m],
                device_id={"pipe": other},
                device_id_type=MESH,
            )
            for m, ref in enumerate((xs, small))
        ]

    def spread_ids():
        id_copy.wait()
        lane = lax.broadcasted_iota(jnp.int32, (1, 128), 1)
        front = back = target = jnp.full((1, 128), -1, jnp.int32)
        ids_own[...] = jnp.full((8, 128), -1, jnp.int32)
        ids_own[0:4, 0:33] = ids_ref[...]
        for m in range(4):
            row = ids_own[m : m + 1, :]
            is_front = row < 2 * n_items
            for above in (2 * n_items, n_items):
                row = jnp.where(row >= above, row - above, row)
            fronts = jnp.where(is_front, row, -1)
            backs = jnp.where(is_front, -1, row)
            here = lane // 32 == m
            front = jnp.where(here, pltpu.roll(fronts, 32 * m, 1) if m else fronts, front)
            back = jnp.where(here, pltpu.roll(backs, 32 * m, 1) if m else backs, back)
            target = jnp.where(here, pltpu.roll(row, (32 * m + 127) % 128, 1), target)
        ids_own[0:1, :] = front
        ids_own[1:2, :] = back
        ids_own[2:3, :] = target
        ids_all[d] = ids_own[...]

        def send(peer, place):
            pltpu.make_async_remote_copy(
                src_ref=ids_own,
                dst_ref=ids_all.at[d],
                send_sem=ids_send,
                recv_sem=ids_recv,
                device_id={"dp": peer},
                device_id_type=MESH,
            ).start()

        each_peer(send)

    def spread(ph, n, for_other=False):
        c, kind = cs[ph], ph // 2
        box = 2 if for_other else c
        narrow, broad = small.at[ph, n], xs.at[ph, n]
        narrow, broad = narrow[...], broad[...].astype(F32)
        hidden = narrow.shape[1] // 2
        top = jnp.concatenate([narrow[:, :hidden], narrow[:, hidden:]], axis=0).astype(BF16)
        wide = jnp.concatenate([broad, broad[:, :128]], axis=1)
        for j in range(half_dp):
            sbuf[box, kind, j, 0:16, :] = top
            sbuf[box, kind, j, 16:32, :] = wide[:, share * j : share * j + 128].astype(BF16)

        def send(peer, place):
            pltpu.make_async_remote_copy(
                src_ref=sbuf.at[box, kind, place],
                dst_ref=rbuf.at[c, kind, d],
                send_sem=x_send.at[box, kind],
                recv_sem=x_recv.at[c, kind],
                device_id={"pipe": other, "dp": peer} if for_other else {"dp": peer},
                device_id_type=MESH,
            ).start()

        each_peer(send, 1 if for_other else 0)
        if not for_other:
            rbuf[c, kind, d] = sbuf[c, kind, block]

    def all_here(c, kind):
        def these(number):
            many(rbuf.at[c, kind, pl.ds(0, number)], x_recv.at[c, kind]).wait()

        if kind == 0:
            these(n_dp - 1)
        else:

            @pl.when(spared & (c == c1))
            def _():
                these(n_dp)

            @pl.when(jnp.logical_not(spared & (c == c1)))
            def _():
                these(n_dp - 1)

    def many(ref, sem):
        return pltpu.make_async_copy(ref, ref, sem)

    def project(x2, j, weights, w, sums):
        low, high = sums
        low = low + mm(x2, weights[w, piece * j : piece * (j + 1), :])
        high = high + mm(x2, weights[w, half + piece * j : half + piece * (j + 1), :])
        return low, high

    def branch(parts, j):
        low = high = 0.0
        for narrow, weights, w in parts:
            low = low + mm(narrow, weights[w, :, piece * j : piece * (j + 1)])
            high = high + mm(narrow, weights[w, :, half + piece * j : half + piece * (j + 1)])
        return jnp.concatenate([low[:8], high[8:]], axis=0)

    def add_branch(out, x, parts, sent=None):
        for j in pieces:
            at = piece_at(j)
            out[:, at] = (x[:, at].astype(F32) + branch(parts, j)).astype(BF16)
            if sent is not None:
                sent(j)

    def activate(pre, w):
        logistic = 0.5 + 0.5 * jnp.tanh(0.5 * pre)
        slopes[w] = logistic * (1.0 + pre * (1.0 - logistic))
        return pre * logistic

    def nothing():
        zeros = jnp.zeros((16, w_in.shape[2]), F32)
        return zeros, zeros

    def gather(sums):
        return sums[0][:8] + sums[1][8:]

    def forward_one(n):
        sums = nothing()
        for j in pieces:
            sums = project(xs[0, n, :, piece_at(j)], j, w_in, c1, sums)
        act = activate(gather(sums), c1)
        small[0, n] = act
        return [(twice(act), w_out, c1)]

    def forward_pair(ph, arrived, sent):
        a, b = pairs[ph]
        sums_a, sums_b = nothing(), nothing()
        for j in pieces:
            arrived(j)
            x2 = xs[ph, 0, :, piece_at(j)]
            sums_a = project(x2, j, w_in, a, sums_a)
            sums_b = project(x2, j, w_in, b, sums_b)
        act_a = activate(gather(sums_a), a)
        small[ph, 0] = act_a
        act_a = twice(act_a)
        act_b = activate(gather(sums_b) + mm(act_a, m_fwd[ph])[:8], b)
        small[ph, 1] = act_b
        parts = [(act_a, w_out, a), (twice(act_b), w_out, b)]

        def onward():
            add_branch(give.at[ph], xs.at[ph, 0], parts, sent)

        if ph == 0:
            onward()
        else:
            pl.when(k > 0)(onward)

    def backward_sums(ph, arrived):
        a, b = pairs[3 - ph]
        sums_a, sums_b = nothing(), nothing()
        for j in pieces:
            arrived(j)
            g2 = xs[ph, 0, :, piece_at(j)]
            sums_b = project(g2, j, t_out, b, sums_b)
            sums_a = project(g2, j, t_out, a, sums_a)
        bases[0] = gather(sums_a)
        bases[1] = gather(sums_b)

    def backward_pair(ph):
        a, b = pairs[3 - ph]
        grad_b = bases[1] * slopes[b]
        small[ph, 0] = grad_b
        grad_b = twice(grad_b)
        grad_a = (bases[0] + mm(grad_b, m_bwd[3 - ph])[:8]) * slopes[a]
        small[ph, 1] = grad_a
        return [(grad_b, t_in, b), (twice(grad_a), t_in, a)]

    def between(blk):
        a, b = pairs[blk]
        both = mm(w_out[a], w_in[b])
        m_fwd[blk] = both.astype(BF16)
        m_bwd[blk] = both.T.astype(BF16)

    def turn(w):
        tile = w_in.shape[2]

        def one(n, carry):
            at = pl.ds(pl.multiple_of(n * tile, tile), tile)
            t_in[w, :, at] = w_in[w, at, :].T
            t_out[w, at, :] = w_out[w, :, at].T
            return carry

        lax.fori_loop(0, 2 * half // tile, one, 0)

    def unpack(c, kind):
        all_here(c, kind)
        rows = rbuf[c, kind].astype(F32)
        flat = lambda part: part.reshape(n_dp * 8, 128)
        narrow = jnp.concatenate([flat(rows[:, 0:8]), flat(rows[:, 8:16])], axis=1)
        broad = jnp.where(path == 0, flat(rows[:, 16:24]), flat(rows[:, 24:32]))
        return narrow.astype(BF16), broad

    def prepare():
        for c in (0, 1):
            act, x = unpack(c, 0)
            act_rows[c] = act
            x_turned[c] = x.T.astype(BF16)

    def finish(c):
        grad_pre, grad_y = unpack(c, 1)
        gin_ref[0, c] = mm(x_turned[c], grad_pre)[:share]
        gout_ref[0, c] = mm(grad_y.T.astype(BF16), act_rows[c])[:share]

    early = 1 - chip // (chips // 2)

    def seeds():
        all_rows.wait()
        mine = lax.broadcasted_iota(jnp.int32, (16, 128), 0) + 8 * block
        every = lax.broadcasted_iota(jnp.int32, (128, 128), 0)

        def count(group, total):
            left, right = [], []
            for n in range(8):
                tile = ids_all[group * 8 + n]
                events = jnp.where(path == 0, tile[0:1, :], tile[1:2, :])
                left.append(jnp.where(mine == events, 1.0, 0.0).astype(BF16))
                right.append(jnp.where(every == tile[2:3, :], 1.0, 0.0).astype(BF16))
            return total + mm_t(jnp.concatenate(left, axis=1), jnp.concatenate(right, axis=1))

        counts = lax.fori_loop(0, n_dp // 8, count, jnp.zeros((16, 128), F32))[:8]
        sixteens = jnp.floor(counts * 0.0625)
        parts = jnp.concatenate([sixteens, counts - 16.0 * sixteens], axis=0).astype(BF16)
        sums = mm(parts, cand_ref[...])
        xs[2, 0] = fold((16.0 * sums[:8] + sums[8:]) * scale).astype(BF16)

    @pl.when(starts & (k == 0))
    def _():
        own_rows.wait()
        rows = first_rows[...].astype(F32)
        mine = jnp.where(block % 2 == 0, rows[:8], rows[8:])
        xs[0, 0] = fold(mine).astype(BF16)
        for copy in load(c1):
            copy.wait()
        add_branch(xs.at[0, 1], xs.at[0, 0], forward_one(0))

    @pl.when(relay & (k > 0) & (k < last))
    def _():
        pl.semaphore_wait(barrier, 8)

    @pl.when(relay & edge)
    def _():
        pl.semaphore_wait(barrier, 7)

    @pl.when(jnp.logical_not(relay))
    def _():
        pl.semaphore_wait(barrier, 1)

    @pl.when(k == 0)
    def _():
        @pl.when(starts)
        def _():
            pass_on().start()

        @pl.when(jnp.logical_not(starts))
        def _():
            for copy in load(c1):
                copy.wait()
            pass_on().wait_recv()
            add_branch(
                give.at[0], xs.at[0, 1], forward_one(1), lambda j: hop(0, j, up).start()
            )

    @pl.when(jnp.logical_not(relay))
    def _():
        @pl.when(k == 0)
        def _():
            back().start()

        for copy in lend(c1):
            copy.start()
        for copy in lend(c1):
            copy.wait_send()
        for copy in lend(c2):
            copy.start()

        @pl.when(k > 0)
        def _():
            for copy in mail(0):
                copy.wait_recv()

        pl.semaphore_wait(met.at[5], 1)
        spread(0, 1 - own(0))
        for ph in (1, 2):
            for copy in mail(ph):
                copy.wait_recv()
            spread(ph, 1 - own(ph))
        prepare()

        @pl.when(k == 0)
        def _():
            finish(early)

        @pl.when(k > 0)
        def _():
            for copy in mail(3):
                copy.wait_recv()
            spread(3, 1 - own(3))
            finish(early)

        finish(1 - early)
        for copy in lend(c2):
            copy.wait_send()

        @pl.when(k == 0)
        def _():
            back().wait_send()

    @pl.when(relay)
    def _():
        def from_below(ph):
            def wait(j):
                @pl.when(k > 0)
                def _():
                    hop(ph, j, down).wait_recv()

            return wait

        def from_above(ph):
            def wait(j):
                @pl.when(k < last)
                def _():
                    hop(ph, j, up).wait_recv()

            return wait

        def to_above(ph):
            def send(j):
                @pl.when(k < last)
                def _():
                    hop(ph, j, up).start()

            return send

        def to_below(ph):
            def send(j):
                @pl.when(k > 0)
                def _():
                    hop(ph, j, down).start()

            return send

        def lent(blk):
            for copy in lend((c1, c2)[blk]):
                copy.wait_recv()

        def middle(ph):
            w = pairs[ph][0] if ph < 2 else pairs[3 - ph][1]
            weights = w_out if ph < 2 else t_in
            add_branch(xs.at[ph, 1], xs.at[ph, 0], [(twice(small[ph, 0]), weights, w)])

        def post(ph):
            for copy in mail(ph):
                copy.start()

        def settle(ph):
            middle(ph)
            post(ph)
            spread(ph, own(ph))

        def ready(blk):
            for copy in load((c1, c2)[blk]):
                copy.wait()

        def turn_and_meet():
            turn(c1)
            met_by(0)
            ready(1)
            turn(c2)
            met_by(1)

            @pl.when(k == 0)
            def _():
                lent(0)

            turn(2 + c1)
            met_by(2)
            lent(1)
            turn(2 + c2)
            met_by(3)

        @pl.when(k == 0)
        def _():
            meet(0, rounds[0])
            turn_and_meet()
            meet_other_plane()
            spread_ids()
            spread(0, own(0))
            between(0)
            between(1)
            many(ids_all.at[pl.ds(0, n_dp - 1)], ids_recv).wait()
            seeds()
            backward_sums(2, lambda j: None)
            back().wait_recv()

        @pl.when(k > 0)
        def _():
            meet(0, rounds[0])
            ready(0)
            lent(0)
            between(0)

            @pl.when(k > 1)
            def _():
                met_by(0)

            @pl.when(k == last)
            def _():
                met_by(1)
                met_by(2)
                met_by(3)
                ready(1)
                lent(1)
                between(1)

            forward_pair(0, from_below(0), to_above(0))

            @pl.when(k == last)
            def _():
                xs[1, 0] = give[0]

            @pl.when(k == 1)
            def _():
                turn_and_meet()
                between(1)
                meet_other_plane()
                settle(0)

            @pl.when((k > 1) & (k < last))
            def _():
                met_by(1)
                met_by(2)
                met_by(3)
                ready(1)
                lent(1)
                between(1)

        forward_pair(1, from_above(1), to_below(1))

        @pl.when(k > 0)
        def _():
            @pl.when(k > 1)
            def _():
                meet_other_plane()

                @pl.when(k == last)
                def _():
                    spread_ids()

            settle(1)

            @pl.when(k > 1)
            def _():
                settle(0)
                for w in range(4):
                    turn(w)

        @pl.when(k > 0)
        def _():
            backward_sums(2, lambda j: hop(2, j, down).wait_recv())

        parts = backward_pair(2)
        add_branch(give.at[2], xs.at[2, 0], parts, to_above(2))

        @pl.when(k < last)
        def _():
            @pl.when(k == 0)
            def _():
                settle(1)

            settle(2)
            prepare()

            @pl.when(k == 0)
            def _():
                finish(early)

        @pl.when(k == last)
        def _():
            xs[3, 0] = give[2]

        backward_sums(3, from_above(3))
        parts = backward_pair(3)

        @pl.when(k > 0)
        def _():
            add_branch(give.at[3], xs.at[3, 0], parts, to_below(3))
            settle(3)

        @pl.when(k == 0)
        def _():
            @pl.when(path == 0)
            def _():
                spread(3, 0)
                middle(3)
                spread(3, 1, True)

            @pl.when(path == 1)
            def _():
                spread(3, 0, True)
                middle(3)
                spread(3, 1)

        @pl.when(k == last)
        def _():
            settle(2)
            prepare()

        @pl.when(k > 0)
        def _():
            finish(early)

        finish(1 - early)

        @pl.when(k < last)
        def _():
            for j in pieces:
                hop(2, j, up).wait_send()

        @pl.when((k > 0) & (k < last))
        def _():
            for j in pieces:
                hop(0, j, up).wait_send()

        @pl.when(k > 0)
        def _():
            for j in pieces:
                hop(1, j, down).wait_send()
                hop(3, j, down).wait_send()
            for ph in (0, 3):
                for copy in mail(ph):
                    copy.wait_send()

        for ph in (1, 2):
            for copy in mail(ph):
                copy.wait_send()

        @pl.when(k == 0)
        def _():
            many(rbuf.at[0, 0], x_send.at[2, 1]).wait()

        @pl.when(k == last)
        def _():
            many(ids_all.at[pl.ds(0, n_dp - 1)], ids_recv).wait()

        @pl.when(edge)
        def _():
            many(ids_all.at[pl.ds(0, n_dp - 1)], ids_send).wait()

    @pl.when(k == 0)
    def _():
        @pl.when(starts)
        def _():
            pass_on().wait_send()

        @pl.when(jnp.logical_not(starts))
        def _():
            for j in pieces:
                hop(0, j, up).wait_send()

    def gone(c, kind):
        many(rbuf.at[c, kind, pl.ds(0, n_dp - 1)], x_send.at[c, kind]).wait()

    for ph in range(3):
        gone(cs[ph], ph // 2)

    @pl.when(jnp.logical_not(spared))
    def _():
        gone(cs[3], 1)


def local(n_pipe, n_dp, item_ids, plan_order, candidates, adapters_in, adapters_out):
    batches, width = item_ids.shape
    events = width - 1
    _, _, features, hidden = adapters_in.shape
    share = features // n_dp
    scale = 1.0 / math.sqrt(batches * n_dp * events)
    ids = item_ids + candidates.shape[0] * plan_order[:, None]
    vmem = pl.BlockSpec(memory_space=pltpu.VMEM)
    hbm = pl.BlockSpec(memory_space=pltpu.HBM)
    grad_in, grad_out = pl.pallas_call(
        functools.partial(kernel, n_pipe, n_dp, scale),
        out_shape=(
            jax.ShapeDtypeStruct((1, 2, share, hidden), F32),
            jax.ShapeDtypeStruct((1, 2, share, hidden), F32),
        ),
        in_specs=[hbm] * 4,
        out_specs=(vmem, vmem),
        scratch_shapes=[
            pltpu.VMEM((4, features, hidden), BF16),
            pltpu.VMEM((4, hidden, features), BF16),
            pltpu.VMEM((4, hidden, features), BF16),
            pltpu.VMEM((4, features, hidden), BF16),
            pltpu.VMEM((2, hidden, hidden), BF16),
            pltpu.VMEM((2, hidden, hidden), BF16),
            pltpu.VMEM(ids.shape, jnp.int32),
            pltpu.VMEM(candidates.shape, BF16),
            pltpu.VMEM((16, features), BF16),
            pltpu.VMEM((8, 128), jnp.int32),
            pltpu.VMEM((n_dp, 8, 128), jnp.int32),
            pltpu.VMEM((4, 2, 16, features // 2), BF16),
            pltpu.VMEM((4, 16, features // 2), BF16),
            pltpu.VMEM((4, 2, 8, hidden), F32),
            pltpu.VMEM((4, 8, hidden), F32),
            pltpu.VMEM((2, 8, hidden), F32),
            pltpu.VMEM((3, 2, n_dp // 2, 32, 128), BF16),
            pltpu.VMEM((2, 2, n_dp, 32, 128), BF16),
            pltpu.VMEM((2, 128, n_dp * 8), BF16),
            pltpu.VMEM((2, n_dp * 8, hidden), BF16),
            pltpu.SemaphoreType.DMA((2, 2)),
            pltpu.SemaphoreType.DMA((3,)),
            pltpu.SemaphoreType.DMA((2, 2)),
            pltpu.SemaphoreType.DMA((2, 2)),
            pltpu.SemaphoreType.DMA((4, PIECES)),
            pltpu.SemaphoreType.DMA((4, PIECES)),
            pltpu.SemaphoreType.DMA((4, 2)),
            pltpu.SemaphoreType.DMA((4, 2)),
            pltpu.SemaphoreType.DMA,
            pltpu.SemaphoreType.DMA,
            pltpu.SemaphoreType.DMA,
            pltpu.SemaphoreType.DMA,
            pltpu.SemaphoreType.DMA,
            pltpu.SemaphoreType.DMA,
            pltpu.SemaphoreType.DMA((3, 2)),
            pltpu.SemaphoreType.DMA((2, 2)),
            pltpu.SemaphoreType.REGULAR((6,)),
        ],
        compiler_params=pltpu.CompilerParams(
            collective_id=0, has_side_effects=True, vmem_limit_bytes=107 * 512 * 1024
        ),
    )(ids, candidates, adapters_in, adapters_out)
    return grad_in, jnp.swapaxes(grad_out, 2, 3)


def solution(mesh):
    in_specs = (P(None, "dp"), P(), P(), P("pipe", None, None, None), P("pipe", None, None, None))
    out_specs = (P("pipe", None, "dp", None), P("pipe", None, None, "dp"))
    return jax.shard_map(
        functools.partial(local, mesh.shape["pipe"], mesh.shape["dp"]),
        mesh=mesh,
        in_specs=in_specs,
        out_specs=out_specs,
        check_vma=False,
    )
```

```python
import functools
import math

import jax
import jax.numpy as jnp
from jax import lax
from jax.experimental import pallas as pl
from jax.experimental.pallas import tpu as pltpu
from jax.sharding import PartitionSpec as P

MESH = pl.DeviceIdType.MESH
F32 = jnp.float32
BF16 = jnp.bfloat16
PIECES = 3


def mm(a, b):
    return jnp.dot(a, b, preferred_element_type=F32)


def mm_t(a, b):
    return lax.dot_general(a, b, (((1,), (1,)), ((), ())), preferred_element_type=F32)


def t_mm(a, b):
    return lax.dot_general(a, b, (((0,), (0,)), ((), ())), preferred_element_type=F32)


def fold(wide):
    half = wide.shape[1] // 2
    return jnp.concatenate([wide[:, :half], wide[:, half:]], axis=0)


def twice(rows):
    return jnp.concatenate([rows, rows], axis=0).astype(BF16)


def kernel(
    n_pipe,
    n_dp,
    scale,
    ids_hbm,
    cand_hbm,
    win_ref,
    wout_ref,
    gin_ref,
    gout_ref,
    w_in,
    w_out,
    t_in,
    t_out,
    m_fwd,
    m_bwd,
    ids_ref,
    cand_ref,
    first_rows,
    ids_own,
    ids_all,
    xs,
    give,
    small,
    slopes,
    bases,
    sbuf,
    rbuf,
    x_turned,
    act_rows,
    w_sem,
    cand_sem,
    share_send,
    share_recv,
    give_sem,
    got_sem,
    mail_send,
    mail_recv,
    pass_send,
    pass_recv,
    back_send,
    back_recv,
    ids_send,
    ids_recv,
    x_send,
    x_recv,
    met,
):
    p = lax.axis_index("pipe")
    d = lax.axis_index("dp")
    half_dp = n_dp // 2
    path = d // half_dp
    block = d % half_dp
    c1 = path
    c2 = 1 - path
    chips = n_pipe // 2
    chip = p // 2
    core = p % 2
    relay = core == 1
    starts = core == path
    other = p + 1 - 2 * core
    last = chips - 1
    k = chip + path * (last - 2 * chip)
    up = 2 * chip + 3 - 4 * path
    down = 2 * chip - 1 + 4 * path
    edge = (k == 0) | (k == last)
    half = w_in.shape[1] // 2
    piece = half // PIECES
    pieces = range(PIECES)
    pairs = ((c1 + 2 - 2 * path, c1 + 2 * path), (c2 + 2 * path, c2 + 2 - 2 * path))

    spared = (core == 0) & (k == 0)

    def own(ph):
        return (ph + 1 + path) % 2

    share = 2 * half // n_dp
    cs = (c1, c2, c2, c1)

    def load(c):
        return (
            pltpu.make_async_copy(win_ref.at[0, c], w_in.at[c], w_sem.at[c, 0]),
            pltpu.make_async_copy(wout_ref.at[0, c], w_out.at[c], w_sem.at[c, 1]),
        )

    def lend(c):
        return [
            pltpu.make_async_remote_copy(
                src_ref=src.at[0, c],
                dst_ref=dst.at[2 + c],
                send_sem=share_send.at[c, n],
                recv_sem=share_recv.at[c, n],
                device_id={"pipe": other},
                device_id_type=MESH,
            )
            for n, (src, dst) in enumerate(((win_ref, w_in), (wout_ref, w_out)))
        ]

    start = pl.multiple_of(16 * (block // 2), 16)
    own_rows = pltpu.make_async_copy(cand_hbm.at[pl.ds(start, 16)], first_rows, cand_sem.at[0])
    all_rows = pltpu.make_async_copy(cand_hbm, cand_ref, cand_sem.at[1])

    id_copy = pltpu.make_async_copy(ids_hbm, ids_ref, cand_sem.at[2])

    @pl.when(starts & (k == 0))
    def _():
        own_rows.start()

    @pl.when(relay | (k == 0))
    def _():
        for copy in load(c1):
            copy.start()

    @pl.when(relay)
    def _():
        @pl.when(edge)
        def _():
            id_copy.start()

        for copy in load(c2):
            copy.start()

        @pl.when(k == 0)
        def _():
            all_rows.start()

    side, row, column = d // 16, (d // 4) % 4, d % 4
    planes = [16 * ((side + 1) % 2), 16 * side]
    columns = [(column + away) % 4 for away in (2, 1, 3, 0)]

    def each_peer(do, too=0):
        def line(n, carry):
            at = 4 * ((row + (2 + 3 * (n * (n + 1) // 2)) % 4) % 4)
            for x in columns:
                for z in planes:
                    do(z + at + x, at + x)
            return carry

        lax.fori_loop(0, 3, line, 0)
        near = [(z, x) for x in columns for z in planes]
        for z, x in near[: 7 + too]:
            do(z + 4 * row + x, 4 * row + x)

    barrier = pltpu.get_barrier_semaphore()

    def hello(to):
        pl.semaphore_signal(barrier, inc=1, device_id={"pipe": to}, device_id_type=MESH)

    hello(other)

    @pl.when(relay & (k < last))
    def _():
        hello(up)

    @pl.when(relay & (k > 0))
    def _():
        hello(down)

    beside = [16 * side + 4 * row + (column + step) % 4 for step in (1, 3)]
    above = [16 * side + 4 * ((row + step) % 4) + column for step in (1, 3)]
    facing = 16 * ((side + 1) % 2) + 4 * row + column

    @pl.when(relay)
    def _():
        for peer in (*beside, *above, facing):
            pl.semaphore_signal(barrier, inc=1, device_id={"dp": peer}, device_id_type=MESH)

    def meet(n, peers):
        for peer in peers:
            pl.semaphore_signal(met.at[n], inc=1, device_id={"dp": peer}, device_id_type=MESH)

    rounds = (beside, beside, above, above, [facing])

    def met_by(n):
        pl.semaphore_wait(met.at[n], 2)
        meet(n + 1, rounds[n + 1])

    def meet_other_plane():
        pl.semaphore_wait(met.at[4], 1)
        pl.semaphore_signal(met.at[5], inc=1, device_id={"pipe": other}, device_id_type=MESH)

    def piece_at(j):
        return pl.ds(j * piece, piece)

    def hop(ph, j, to):
        return pltpu.make_async_remote_copy(
            src_ref=give.at[ph, :, piece_at(j)],
            dst_ref=xs.at[ph, 0, :, piece_at(j)],
            send_sem=give_sem.at[ph, j],
            recv_sem=got_sem.at[ph, j],
            device_id={"pipe": to},
            device_id_type=MESH,
        )

    def back():
        return pltpu.make_async_remote_copy(
            src_ref=slopes.at[c1],
            dst_ref=slopes.at[2 + c1],
            send_sem=back_send,
            recv_sem=back_recv,
            device_id={"pipe": other},
            device_id_type=MESH,
        )

    def pass_on():
        return pltpu.make_async_remote_copy(
            src_ref=xs.at[0, 1],
            dst_ref=xs.at[0, 1],
            send_sem=pass_send,
            recv_sem=pass_recv,
            device_id={"pipe": other},
            device_id_type=MESH,
        )

    def mail(ph):
        n = 1 - own(ph)
        return [
            pltpu.make_async_remote_copy(
                src_ref=ref.at[ph, n],
                dst_ref=ref.at[ph, n],
                send_sem=mail_send.at[ph, m],
                recv_sem=mail_recv.at[ph, m],
                device_id={"pipe": other},
                device_id_type=MESH,
            )
            for m, ref in enumerate((xs, small))
        ]

    def spread_ids():
        id_copy.wait()
        lane = lax.broadcasted_iota(jnp.int32, (1, 128), 1)
        front = back = target = jnp.full((1, 128), -1, jnp.int32)
        ids_own[...] = jnp.full((8, 128), -1, jnp.int32)
        ids_own[0:5, 0:33] = ids_ref[...]
        plan = ids_own[4:5, :]
        for m in range(4):
            row = ids_own[m : m + 1, :]
            is_front = plan[:, m : m + 1] < 2
            fronts = jnp.where(is_front, row, -1)
            backs = jnp.where(is_front, -1, row)
            here = lane // 32 == m
            front = jnp.where(here, pltpu.roll(fronts, 32 * m, 1) if m else fronts, front)
            back = jnp.where(here, pltpu.roll(backs, 32 * m, 1) if m else backs, back)
            target = jnp.where(here, pltpu.roll(row, (32 * m + 127) % 128, 1), target)
        ids_own[0:1, :] = front
        ids_own[1:2, :] = back
        ids_own[2:3, :] = target
        ids_all[d] = ids_own[...]

        def send(peer, place):
            pltpu.make_async_remote_copy(
                src_ref=ids_own,
                dst_ref=ids_all.at[d],
                send_sem=ids_send,
                recv_sem=ids_recv,
                device_id={"dp": peer},
                device_id_type=MESH,
            ).start()

        each_peer(send)

    def spread(ph, n, for_other=False):
        c, kind = cs[ph], ph // 2
        box = 2 if for_other else c
        narrow, broad = small.at[ph, n], xs.at[ph, n]
        narrow, broad = narrow[...], broad[...].astype(F32)
        hidden = narrow.shape[1] // 2
        top = jnp.concatenate([narrow[:, :hidden], narrow[:, hidden:]], axis=0).astype(BF16)
        wide = jnp.concatenate([broad, broad[:, :128]], axis=1)
        for j in range(half_dp):
            sbuf[box, kind, j, 0:16, :] = top
            sbuf[box, kind, j, 16:32, :] = wide[:, share * j : share * j + 128].astype(BF16)

        def send(peer, place):
            pltpu.make_async_remote_copy(
                src_ref=sbuf.at[box, kind, place],
                dst_ref=rbuf.at[c, kind, d],
                send_sem=x_send.at[box, kind],
                recv_sem=x_recv.at[c, kind],
                device_id={"pipe": other, "dp": peer} if for_other else {"dp": peer},
                device_id_type=MESH,
            ).start()

        each_peer(send, 1 if for_other else 0)
        if not for_other:
            rbuf[c, kind, d] = sbuf[c, kind, block]

    def all_here(c, kind):
        def these(number):
            many(rbuf.at[c, kind, pl.ds(0, number)], x_recv.at[c, kind]).wait()

        if kind == 0:
            these(n_dp - 1)
        else:

            @pl.when(spared & (c == c1))
            def _():
                these(n_dp)

            @pl.when(jnp.logical_not(spared & (c == c1)))
            def _():
                these(n_dp - 1)

    def many(ref, sem):
        return pltpu.make_async_copy(ref, ref, sem)

    def project(x2, j, weights, w, sums):
        low, high = sums
        low = low + mm(x2, weights[w, piece * j : piece * (j + 1), :])
        high = high + mm(x2, weights[w, half + piece * j : half + piece * (j + 1), :])
        return low, high

    def branch(parts, j):
        low = high = 0.0
        for narrow, weights, w in parts:
            low = low + mm(narrow, weights[w, :, piece * j : piece * (j + 1)])
            high = high + mm(narrow, weights[w, :, half + piece * j : half + piece * (j + 1)])
        return jnp.concatenate([low[:8], high[8:]], axis=0)

    def add_branch(out, x, parts, sent=None):
        for j in pieces:
            at = piece_at(j)
            out[:, at] = (x[:, at].astype(F32) + branch(parts, j)).astype(BF16)
            if sent is not None:
                sent(j)

    def activate(pre, w):
        logistic = 0.5 + 0.5 * jnp.tanh(0.5 * pre)
        slopes[w] = logistic * (1.0 + pre * (1.0 - logistic))
        return pre * logistic

    def nothing():
        zeros = jnp.zeros((16, w_in.shape[2]), F32)
        return zeros, zeros

    def gather(sums):
        return sums[0][:8] + sums[1][8:]

    def forward_one(n):
        sums = nothing()
        for j in pieces:
            sums = project(xs[0, n, :, piece_at(j)], j, w_in, c1, sums)
        act = activate(gather(sums), c1)
        small[0, n] = act
        return [(twice(act), w_out, c1)]

    def forward_pair(ph, arrived, sent):
        a, b = pairs[ph]
        sums_a, sums_b = nothing(), nothing()
        for j in pieces:
            arrived(j)
            x2 = xs[ph, 0, :, piece_at(j)]
            sums_a = project(x2, j, w_in, a, sums_a)
            sums_b = project(x2, j, w_in, b, sums_b)
        act_a = activate(gather(sums_a), a)
        small[ph, 0] = act_a
        act_a = twice(act_a)
        act_b = activate(gather(sums_b) + mm(act_a, m_fwd[ph])[:8], b)
        small[ph, 1] = act_b
        parts = [(act_a, w_out, a), (twice(act_b), w_out, b)]

        def onward():
            add_branch(give.at[ph], xs.at[ph, 0], parts, sent)

        if ph == 0:
            onward()
        else:
            pl.when(k > 0)(onward)

    def backward_sums(ph, arrived):
        a, b = pairs[3 - ph]
        sums_a, sums_b = nothing(), nothing()
        for j in pieces:
            arrived(j)
            g2 = xs[ph, 0, :, piece_at(j)]
            sums_b = project(g2, j, t_out, b, sums_b)
            sums_a = project(g2, j, t_out, a, sums_a)
        bases[0] = gather(sums_a)
        bases[1] = gather(sums_b)

    def backward_pair(ph):
        a, b = pairs[3 - ph]
        grad_b = bases[1] * slopes[b]
        small[ph, 0] = grad_b
        grad_b = twice(grad_b)
        grad_a = (bases[0] + mm(grad_b, m_bwd[3 - ph])[:8]) * slopes[a]
        small[ph, 1] = grad_a
        return [(grad_b, t_in, b), (twice(grad_a), t_in, a)]

    def between(blk):
        a, b = pairs[blk]
        both = mm(w_out[a], w_in[b])
        m_fwd[blk] = both.astype(BF16)
        m_bwd[blk] = both.T.astype(BF16)

    def turn(w):
        tile = w_in.shape[2]

        def one(n, carry):
            at = pl.ds(pl.multiple_of(n * tile, tile), tile)
            t_in[w, :, at] = w_in[w, at, :].T
            t_out[w, at, :] = w_out[w, :, at].T
            return carry

        lax.fori_loop(0, 2 * half // tile, one, 0)

    def unpack(c, kind):
        all_here(c, kind)
        rows = rbuf[c, kind].astype(F32)
        flat = lambda part: part.reshape(n_dp * 8, 128)
        narrow = jnp.concatenate([flat(rows[:, 0:8]), flat(rows[:, 8:16])], axis=1)
        broad = jnp.where(path == 0, flat(rows[:, 16:24]), flat(rows[:, 24:32]))
        return narrow.astype(BF16), broad

    def prepare():
        for c in (0, 1):
            act, x = unpack(c, 0)
            act_rows[c] = act
            x_turned[c] = x.T.astype(BF16)

    def finish(c):
        grad_pre, grad_y = unpack(c, 1)
        gin_ref[0, c] = mm(x_turned[c], grad_pre)[:share]
        gout_ref[0, c] = mm(grad_y.T.astype(BF16), act_rows[c])[:share]

    early = 1 - chip // (chips // 2)

    def seeds():
        all_rows.wait()
        mine = lax.broadcasted_iota(jnp.int32, (16, 128), 0) + 8 * block
        every = lax.broadcasted_iota(jnp.int32, (128, 128), 0)

        def count(group, total):
            left, right = [], []
            for n in range(8):
                tile = ids_all[group * 8 + n]
                events = jnp.where(path == 0, tile[0:1, :], tile[1:2, :])
                left.append(jnp.where(mine == events, 1.0, 0.0).astype(BF16))
                right.append(jnp.where(every == tile[2:3, :], 1.0, 0.0).astype(BF16))
            return total + mm_t(jnp.concatenate(left, axis=1), jnp.concatenate(right, axis=1))

        counts = lax.fori_loop(0, n_dp // 8, count, jnp.zeros((16, 128), F32))[:8]
        sixteens = jnp.floor(counts * 0.0625)
        parts = jnp.concatenate([sixteens, counts - 16.0 * sixteens], axis=0).astype(BF16)
        sums = mm(parts, cand_ref[...])
        xs[2, 0] = fold((16.0 * sums[:8] + sums[8:]) * scale).astype(BF16)

    @pl.when(starts & (k == 0))
    def _():
        own_rows.wait()
        rows = first_rows[...].astype(F32)
        mine = jnp.where(block % 2 == 0, rows[:8], rows[8:])
        xs[0, 0] = fold(mine).astype(BF16)
        for copy in load(c1):
            copy.wait()
        add_branch(xs.at[0, 1], xs.at[0, 0], forward_one(0))

    @pl.when(relay & (k > 0) & (k < last))
    def _():
        pl.semaphore_wait(barrier, 8)

    @pl.when(relay & edge)
    def _():
        pl.semaphore_wait(barrier, 7)

    @pl.when(jnp.logical_not(relay))
    def _():
        pl.semaphore_wait(barrier, 1)

    @pl.when(k == 0)
    def _():
        @pl.when(starts)
        def _():
            pass_on().start()

        @pl.when(jnp.logical_not(starts))
        def _():
            for copy in load(c1):
                copy.wait()
            pass_on().wait_recv()
            add_branch(
                give.at[0], xs.at[0, 1], forward_one(1), lambda j: hop(0, j, up).start()
            )

    @pl.when(jnp.logical_not(relay))
    def _():
        @pl.when(k == 0)
        def _():
            back().start()

        for copy in lend(c1):
            copy.start()
        for copy in lend(c1):
            copy.wait_send()
        for copy in lend(c2):
            copy.start()

        @pl.when(k > 0)
        def _():
            for copy in mail(0):
                copy.wait_recv()

        pl.semaphore_wait(met.at[5], 1)
        spread(0, 1 - own(0))
        for ph in (1, 2):
            for copy in mail(ph):
                copy.wait_recv()
            spread(ph, 1 - own(ph))
        prepare()

        @pl.when(k == 0)
        def _():
            finish(early)

        @pl.when(k > 0)
        def _():
            for copy in mail(3):
                copy.wait_recv()
            spread(3, 1 - own(3))
            finish(early)

        finish(1 - early)
        for copy in lend(c2):
            copy.wait_send()

        @pl.when(k == 0)
        def _():
            back().wait_send()

    @pl.when(relay)
    def _():
        def from_below(ph):
            def wait(j):
                @pl.when(k > 0)
                def _():
                    hop(ph, j, down).wait_recv()

            return wait

        def from_above(ph):
            def wait(j):
                @pl.when(k < last)
                def _():
                    hop(ph, j, up).wait_recv()

            return wait

        def to_above(ph):
            def send(j):
                @pl.when(k < last)
                def _():
                    hop(ph, j, up).start()

            return send

        def to_below(ph):
            def send(j):
                @pl.when(k > 0)
                def _():
                    hop(ph, j, down).start()

            return send

        def lent(blk):
            for copy in lend((c1, c2)[blk]):
                copy.wait_recv()

        def middle(ph):
            w = pairs[ph][0] if ph < 2 else pairs[3 - ph][1]
            weights = w_out if ph < 2 else t_in
            add_branch(xs.at[ph, 1], xs.at[ph, 0], [(twice(small[ph, 0]), weights, w)])

        def post(ph):
            for copy in mail(ph):
                copy.start()

        def settle(ph):
            middle(ph)
            post(ph)
            spread(ph, own(ph))

        def ready(blk):
            for copy in load((c1, c2)[blk]):
                copy.wait()

        def turn_and_meet():
            turn(c1)
            met_by(0)
            ready(1)
            turn(c2)
            met_by(1)

            @pl.when(k == 0)
            def _():
                lent(0)

            turn(2 + c1)
            met_by(2)
            lent(1)
            turn(2 + c2)
            met_by(3)

        @pl.when(k == 0)
        def _():
            meet(0, rounds[0])
            turn_and_meet()
            meet_other_plane()
            spread_ids()
            spread(0, own(0))
            between(0)
            between(1)
            many(ids_all.at[pl.ds(0, n_dp - 1)], ids_recv).wait()
            seeds()
            backward_sums(2, lambda j: None)
            back().wait_recv()

        @pl.when(k > 0)
        def _():
            meet(0, rounds[0])
            ready(0)
            lent(0)
            between(0)

            @pl.when(k > 1)
            def _():
                met_by(0)

            @pl.when(k == last)
            def _():
                met_by(1)
                met_by(2)
                met_by(3)
                ready(1)
                lent(1)
                between(1)

            forward_pair(0, from_below(0), to_above(0))

            @pl.when(k == last)
            def _():
                xs[1, 0] = give[0]

            @pl.when(k == 1)
            def _():
                turn_and_meet()
                between(1)
                meet_other_plane()
                settle(0)

            @pl.when((k > 1) & (k < last))
            def _():
                met_by(1)
                met_by(2)
                met_by(3)
                ready(1)
                lent(1)
                between(1)

        forward_pair(1, from_above(1), to_below(1))

        @pl.when(k > 0)
        def _():
            @pl.when(k > 1)
            def _():
                meet_other_plane()

                @pl.when(k == last)
                def _():
                    spread_ids()

            settle(1)

            @pl.when(k > 1)
            def _():
                settle(0)
                for w in range(4):
                    turn(w)

        @pl.when(k > 0)
        def _():
            backward_sums(2, lambda j: hop(2, j, down).wait_recv())

        parts = backward_pair(2)
        add_branch(give.at[2], xs.at[2, 0], parts, to_above(2))

        @pl.when(k < last)
        def _():
            @pl.when(k == 0)
            def _():
                settle(1)

            settle(2)
            prepare()

            @pl.when(k == 0)
            def _():
                finish(early)

        @pl.when(k == last)
        def _():
            xs[3, 0] = give[2]

        backward_sums(3, from_above(3))
        parts = backward_pair(3)

        @pl.when(k > 0)
        def _():
            add_branch(give.at[3], xs.at[3, 0], parts, to_below(3))
            settle(3)

        @pl.when(k == 0)
        def _():
            @pl.when(path == 0)
            def _():
                spread(3, 0)
                middle(3)
                spread(3, 1, True)

            @pl.when(path == 1)
            def _():
                spread(3, 0, True)
                middle(3)
                spread(3, 1)

        @pl.when(k == last)
        def _():
            settle(2)
            prepare()

        @pl.when(k > 0)
        def _():
            finish(early)

        finish(1 - early)

        @pl.when(k < last)
        def _():
            for j in pieces:
                hop(2, j, up).wait_send()

        @pl.when((k > 0) & (k < last))
        def _():
            for j in pieces:
                hop(0, j, up).wait_send()

        @pl.when(k > 0)
        def _():
            for j in pieces:
                hop(1, j, down).wait_send()
                hop(3, j, down).wait_send()
            for ph in (0, 3):
                for copy in mail(ph):
                    copy.wait_send()

        for ph in (1, 2):
            for copy in mail(ph):
                copy.wait_send()

        @pl.when(k == 0)
        def _():
            many(rbuf.at[0, 0], x_send.at[2, 1]).wait()

        @pl.when(k == last)
        def _():
            many(ids_all.at[pl.ds(0, n_dp - 1)], ids_recv).wait()

        @pl.when(edge)
        def _():
            many(ids_all.at[pl.ds(0, n_dp - 1)], ids_send).wait()

    @pl.when(k == 0)
    def _():
        @pl.when(starts)
        def _():
            pass_on().wait_send()

        @pl.when(jnp.logical_not(starts))
        def _():
            for j in pieces:
                hop(0, j, up).wait_send()

    def gone(c, kind):
        many(rbuf.at[c, kind, pl.ds(0, n_dp - 1)], x_send.at[c, kind]).wait()

    for ph in range(3):
        gone(cs[ph], ph // 2)

    @pl.when(jnp.logical_not(spared))
    def _():
        gone(cs[3], 1)


def local(n_pipe, n_dp, item_ids, plan_order, candidates, adapters_in, adapters_out):
    batches, width = item_ids.shape
    events = width - 1
    _, _, features, hidden = adapters_in.shape
    share = features // n_dp
    scale = 1.0 / math.sqrt(batches * n_dp * events)
    spare = width - plan_order.shape[0]
    ids = lax.pad(item_ids, 0, ((0, 1, 0), (0, 0, 0))) + lax.pad(
        plan_order[None, :], 0, ((batches, 0, 0), (0, spare, 0))
    )
    vmem = pl.BlockSpec(memory_space=pltpu.VMEM)
    hbm = pl.BlockSpec(memory_space=pltpu.HBM)
    grad_in, grad_out = pl.pallas_call(
        functools.partial(kernel, n_pipe, n_dp, scale),
        out_shape=(
            jax.ShapeDtypeStruct((1, 2, share, hidden), F32),
            jax.ShapeDtypeStruct((1, 2, share, hidden), F32),
        ),
        in_specs=[hbm] * 4,
        out_specs=(vmem, vmem),
        scratch_shapes=[
            pltpu.VMEM((4, features, hidden), BF16),
            pltpu.VMEM((4, hidden, features), BF16),
            pltpu.VMEM((4, hidden, features), BF16),
            pltpu.VMEM((4, features, hidden), BF16),
            pltpu.VMEM((2, hidden, hidden), BF16),
            pltpu.VMEM((2, hidden, hidden), BF16),
            pltpu.VMEM(ids.shape, jnp.int32),
            pltpu.VMEM(candidates.shape, BF16),
            pltpu.VMEM((16, features), BF16),
            pltpu.VMEM((8, 128), jnp.int32),
            pltpu.VMEM((n_dp, 8, 128), jnp.int32),
            pltpu.VMEM((4, 2, 16, features // 2), BF16),
            pltpu.VMEM((4, 16, features // 2), BF16),
            pltpu.VMEM((4, 2, 8, hidden), F32),
            pltpu.VMEM((4, 8, hidden), F32),
            pltpu.VMEM((2, 8, hidden), F32),
            pltpu.VMEM((3, 2, n_dp // 2, 32, 128), BF16),
            pltpu.VMEM((2, 2, n_dp, 32, 128), BF16),
            pltpu.VMEM((2, 128, n_dp * 8), BF16),
            pltpu.VMEM((2, n_dp * 8, hidden), BF16),
            pltpu.SemaphoreType.DMA((2, 2)),
            pltpu.SemaphoreType.DMA((3,)),
            pltpu.SemaphoreType.DMA((2, 2)),
            pltpu.SemaphoreType.DMA((2, 2)),
            pltpu.SemaphoreType.DMA((4, PIECES)),
            pltpu.SemaphoreType.DMA((4, PIECES)),
            pltpu.SemaphoreType.DMA((4, 2)),
            pltpu.SemaphoreType.DMA((4, 2)),
            pltpu.SemaphoreType.DMA,
            pltpu.SemaphoreType.DMA,
            pltpu.SemaphoreType.DMA,
            pltpu.SemaphoreType.DMA,
            pltpu.SemaphoreType.DMA,
            pltpu.SemaphoreType.DMA,
            pltpu.SemaphoreType.DMA((3, 2)),
            pltpu.SemaphoreType.DMA((2, 2)),
            pltpu.SemaphoreType.REGULAR((6,)),
        ],
        compiler_params=pltpu.CompilerParams(
            collective_id=0, has_side_effects=True, vmem_limit_bytes=107 * 512 * 1024
        ),
    )(ids, candidates, adapters_in, adapters_out)
    return grad_in, jnp.swapaxes(grad_out, 2, 3)


def solution(mesh):
    in_specs = (P(None, "dp"), P(), P(), P("pipe", None, None, None), P("pipe", None, None, None))
    out_specs = (P("pipe", None, "dp", None), P("pipe", None, None, "dp"))
    return jax.shard_map(
        functools.partial(local, mesh.shape["pipe"], mesh.shape["dp"]),
        mesh=mesh,
        in_specs=in_specs,
        out_specs=out_specs,
        check_vma=False,
    )
```

```python
import functools
import math

import jax
import jax.numpy as jnp
from jax import lax
from jax.experimental import pallas as pl
from jax.experimental.pallas import tpu as pltpu
from jax.sharding import PartitionSpec as P

MESH = pl.DeviceIdType.MESH
F32 = jnp.float32
BF16 = jnp.bfloat16
PIECES = 3


def mm(a, b):
    return jnp.dot(a, b, preferred_element_type=F32)


def mm_t(a, b):
    return lax.dot_general(a, b, (((1,), (1,)), ((), ())), preferred_element_type=F32)


def t_mm(a, b):
    return lax.dot_general(a, b, (((0,), (0,)), ((), ())), preferred_element_type=F32)


def fold(wide):
    half = wide.shape[1] // 2
    return jnp.concatenate([wide[:, :half], wide[:, half:]], axis=0)


def twice(rows):
    return jnp.concatenate([rows, rows], axis=0).astype(BF16)


def kernel(
    n_pipe,
    n_dp,
    scale,
    ids_hbm,
    cand_hbm,
    win_ref,
    wout_ref,
    gin_ref,
    gout_ref,
    w_in,
    w_out,
    t_in,
    t_out,
    m_fwd,
    m_bwd,
    ids_ref,
    cand_ref,
    first_rows,
    ids_own,
    ids_all,
    xs,
    give,
    small,
    slopes,
    bases,
    sbuf,
    rbuf,
    x_turned,
    act_rows,
    w_sem,
    cand_sem,
    share_send,
    share_recv,
    give_sem,
    got_sem,
    mail_send,
    mail_recv,
    pass_send,
    pass_recv,
    back_send,
    back_recv,
    ids_send,
    ids_recv,
    x_send,
    x_recv,
    met,
):
    p = lax.axis_index("pipe")
    d = lax.axis_index("dp")
    half_dp = n_dp // 2
    path = d // half_dp
    block = d % half_dp
    c1 = path
    c2 = 1 - path
    chips = n_pipe // 2
    chip = p // 2
    core = p % 2
    relay = core == 1
    starts = core == path
    other = p + 1 - 2 * core
    last = chips - 1
    k = chip + path * (last - 2 * chip)
    up = 2 * chip + 3 - 4 * path
    down = 2 * chip - 1 + 4 * path
    edge = (k == 0) | (k == last)
    half = w_in.shape[1] // 2
    piece = half // PIECES
    pieces = range(PIECES)
    pairs = ((c1 + 2 - 2 * path, c1 + 2 * path), (c2 + 2 * path, c2 + 2 - 2 * path))

    spared = (core == 0) & (k == 0)

    def own(ph):
        return (ph + 1 + path) % 2

    share = 2 * half // n_dp
    cs = (c1, c2, c2, c1)

    def load(c):
        return (
            pltpu.make_async_copy(win_ref.at[0, c], w_in.at[c], w_sem.at[c, 0]),
            pltpu.make_async_copy(wout_ref.at[0, c], w_out.at[c], w_sem.at[c, 1]),
        )

    def lend(c):
        return [
            pltpu.make_async_remote_copy(
                src_ref=src.at[0, c],
                dst_ref=dst.at[2 + c],
                send_sem=share_send.at[c, n],
                recv_sem=share_recv.at[c, n],
                device_id={"pipe": other},
                device_id_type=MESH,
            )
            for n, (src, dst) in enumerate(((win_ref, w_in), (wout_ref, w_out)))
        ]

    start = pl.multiple_of(16 * (block // 2), 16)
    own_rows = pltpu.make_async_copy(cand_hbm.at[pl.ds(start, 16)], first_rows, cand_sem.at[0])
    all_rows = pltpu.make_async_copy(cand_hbm, cand_ref, cand_sem.at[1])

    id_copy = pltpu.make_async_copy(ids_hbm, ids_ref, cand_sem.at[2])

    @pl.when(starts & (k == 0))
    def _():
        own_rows.start()

    @pl.when(relay | (k == 0))
    def _():
        for copy in load(c1):
            copy.start()

    @pl.when(relay)
    def _():
        @pl.when(edge)
        def _():
            id_copy.start()

    side, row, column = d // 16, (d // 4) % 4, d % 4
    planes = [16 * ((side + 1) % 2), 16 * side]
    columns = [(column + away) % 4 for away in (2, 1, 3, 0)]

    def each_peer(do, too=0):
        def line(n, carry):
            at = 4 * ((row + (2 + 3 * (n * (n + 1) // 2)) % 4) % 4)
            for x in columns:
                for z in planes:
                    do(z + at + x, at + x)
            return carry

        lax.fori_loop(0, 3, line, 0)
        near = [(z, x) for x in columns for z in planes]
        for z, x in near[: 7 + too]:
            do(z + 4 * row + x, 4 * row + x)

    barrier = pltpu.get_barrier_semaphore()

    def hello(to):
        pl.semaphore_signal(barrier, inc=1, device_id={"pipe": to}, device_id_type=MESH)

    hello(other)

    @pl.when(relay & (k < last))
    def _():
        hello(up)

    @pl.when(relay & (k > 0))
    def _():
        hello(down)

    beside = [16 * side + 4 * row + (column + step) % 4 for step in (1, 3)]
    above = [16 * side + 4 * ((row + step) % 4) + column for step in (1, 3)]
    facing = 16 * ((side + 1) % 2) + 4 * row + column

    @pl.when(relay)
    def _():
        for peer in (*beside, *above, facing):
            pl.semaphore_signal(barrier, inc=1, device_id={"dp": peer}, device_id_type=MESH)

    def meet(n, peers):
        for peer in peers:
            pl.semaphore_signal(met.at[n], inc=1, device_id={"dp": peer}, device_id_type=MESH)

    rounds = (beside, beside, above, above, [facing])

    def met_by(n):
        pl.semaphore_wait(met.at[n], 2)
        meet(n + 1, rounds[n + 1])

    def meet_other_plane():
        pl.semaphore_wait(met.at[4], 1)
        pl.semaphore_signal(met.at[5], inc=1, device_id={"pipe": other}, device_id_type=MESH)

    def piece_at(j):
        return pl.ds(j * piece, piece)

    def hop(ph, j, to):
        return pltpu.make_async_remote_copy(
            src_ref=give.at[ph, :, piece_at(j)],
            dst_ref=xs.at[ph, 0, :, piece_at(j)],
            send_sem=give_sem.at[ph, j],
            recv_sem=got_sem.at[ph, j],
            device_id={"pipe": to},
            device_id_type=MESH,
        )

    def back():
        return pltpu.make_async_remote_copy(
            src_ref=slopes.at[c1],
            dst_ref=slopes.at[2 + c1],
            send_sem=back_send,
            recv_sem=back_recv,
            device_id={"pipe": other},
            device_id_type=MESH,
        )

    def pass_on():
        return pltpu.make_async_remote_copy(
            src_ref=xs.at[0, 1],
            dst_ref=xs.at[0, 1],
            send_sem=pass_send,
            recv_sem=pass_recv,
            device_id={"pipe": other},
            device_id_type=MESH,
        )

    def mail(ph):
        n = 1 - own(ph)
        return [
            pltpu.make_async_remote_copy(
                src_ref=ref.at[ph, n],
                dst_ref=ref.at[ph, n],
                send_sem=mail_send.at[ph, m],
                recv_sem=mail_recv.at[ph, m],
                device_id={"pipe": other},
                device_id_type=MESH,
            )
            for m, ref in enumerate((xs, small))
        ]

    def spread_ids():
        id_copy.wait()
        lane = lax.broadcasted_iota(jnp.int32, (1, 128), 1)
        front = back = target = jnp.full((1, 128), -1, jnp.int32)
        ids_own[...] = jnp.full((8, 128), -1, jnp.int32)
        ids_own[0:5, 0:33] = ids_ref[...]
        plan = ids_own[4:5, :]
        for m in range(4):
            row = ids_own[m : m + 1, :]
            is_front = plan[:, m : m + 1] < 2
            fronts = jnp.where(is_front, row, -1)
            backs = jnp.where(is_front, -1, row)
            here = lane // 32 == m
            front = jnp.where(here, pltpu.roll(fronts, 32 * m, 1) if m else fronts, front)
            back = jnp.where(here, pltpu.roll(backs, 32 * m, 1) if m else backs, back)
            target = jnp.where(here, pltpu.roll(row, (32 * m + 127) % 128, 1), target)
        ids_own[0:1, :] = front
        ids_own[1:2, :] = back
        ids_own[2:3, :] = target
        ids_all[d] = ids_own[...]

        def send(peer, place):
            pltpu.make_async_remote_copy(
                src_ref=ids_own,
                dst_ref=ids_all.at[d],
                send_sem=ids_send,
                recv_sem=ids_recv,
                device_id={"dp": peer},
                device_id_type=MESH,
            ).start()

        each_peer(send)

    def spread(ph, n, for_other=False):
        c, kind = cs[ph], ph // 2
        box = 2 if for_other else c
        narrow, broad = small.at[ph, n], xs.at[ph, n]
        narrow, broad = narrow[...], broad[...].astype(F32)
        hidden = narrow.shape[1] // 2
        top = jnp.concatenate([narrow[:, :hidden], narrow[:, hidden:]], axis=0).astype(BF16)
        wide = jnp.concatenate([broad, broad[:, :128]], axis=1)
        for j in range(half_dp):
            sbuf[box, kind, j, 0:16, :] = top
            sbuf[box, kind, j, 16:32, :] = wide[:, share * j : share * j + 128].astype(BF16)

        def send(peer, place):
            pltpu.make_async_remote_copy(
                src_ref=sbuf.at[box, kind, place],
                dst_ref=rbuf.at[c, kind, d],
                send_sem=x_send.at[box, kind],
                recv_sem=x_recv.at[c, kind],
                device_id={"pipe": other, "dp": peer} if for_other else {"dp": peer},
                device_id_type=MESH,
            ).start()

        each_peer(send, 1 if for_other else 0)
        if not for_other:
            rbuf[c, kind, d] = sbuf[c, kind, block]

    def all_here(c, kind):
        def these(number):
            many(rbuf.at[c, kind, pl.ds(0, number)], x_recv.at[c, kind]).wait()

        if kind == 0:
            these(n_dp - 1)
        else:

            @pl.when(spared & (c == c1))
            def _():
                these(n_dp)

            @pl.when(jnp.logical_not(spared & (c == c1)))
            def _():
                these(n_dp - 1)

    def many(ref, sem):
        return pltpu.make_async_copy(ref, ref, sem)

    def project(x2, j, weights, w, sums):
        low, high = sums
        low = low + mm(x2, weights[w, piece * j : piece * (j + 1), :])
        high = high + mm(x2, weights[w, half + piece * j : half + piece * (j + 1), :])
        return low, high

    def branch(parts, j):
        low = high = 0.0
        for narrow, weights, w in parts:
            low = low + mm(narrow, weights[w, :, piece * j : piece * (j + 1)])
            high = high + mm(narrow, weights[w, :, half + piece * j : half + piece * (j + 1)])
        return jnp.concatenate([low[:8], high[8:]], axis=0)

    def add_branch(out, x, parts, sent=None):
        for j in pieces:
            at = piece_at(j)
            out[:, at] = (x[:, at].astype(F32) + branch(parts, j)).astype(BF16)
            if sent is not None:
                sent(j)

    def activate(pre, w):
        logistic = 0.5 + 0.5 * jnp.tanh(0.5 * pre)
        slopes[w] = logistic * (1.0 + pre * (1.0 - logistic))
        return pre * logistic

    def nothing():
        zeros = jnp.zeros((16, w_in.shape[2]), F32)
        return zeros, zeros

    def gather(sums):
        return sums[0][:8] + sums[1][8:]

    def forward_one(n):
        sums = nothing()
        for j in pieces:
            sums = project(xs[0, n, :, piece_at(j)], j, w_in, c1, sums)
        act = activate(gather(sums), c1)
        small[0, n] = act
        return [(twice(act), w_out, c1)]

    def forward_pair(ph, arrived, sent):
        a, b = pairs[ph]
        sums_a, sums_b = nothing(), nothing()
        for j in pieces:
            arrived(j)
            x2 = xs[ph, 0, :, piece_at(j)]
            sums_a = project(x2, j, w_in, a, sums_a)
            sums_b = project(x2, j, w_in, b, sums_b)
        act_a = activate(gather(sums_a), a)
        small[ph, 0] = act_a
        act_a = twice(act_a)
        act_b = activate(gather(sums_b) + mm(act_a, m_fwd[ph])[:8], b)
        small[ph, 1] = act_b
        parts = [(act_a, w_out, a), (twice(act_b), w_out, b)]

        def onward():
            add_branch(give.at[ph], xs.at[ph, 0], parts, sent)

        if ph == 0:
            onward()
        else:
            pl.when(k > 0)(onward)

    def backward_sums(ph, arrived):
        a, b = pairs[3 - ph]
        sums_a, sums_b = nothing(), nothing()
        for j in pieces:
            arrived(j)
            g2 = xs[ph, 0, :, piece_at(j)]
            sums_b = project(g2, j, t_out, b, sums_b)
            sums_a = project(g2, j, t_out, a, sums_a)
        bases[0] = gather(sums_a)
        bases[1] = gather(sums_b)

    def backward_pair(ph):
        a, b = pairs[3 - ph]
        grad_b = bases[1] * slopes[b]
        small[ph, 0] = grad_b
        grad_b = twice(grad_b)
        grad_a = (bases[0] + mm(grad_b, m_bwd[3 - ph])[:8]) * slopes[a]
        small[ph, 1] = grad_a
        return [(grad_b, t_in, b), (twice(grad_a), t_in, a)]

    def between(blk):
        a, b = pairs[blk]
        both = mm(w_out[a], w_in[b])
        m_fwd[blk] = both.astype(BF16)
        m_bwd[blk] = both.T.astype(BF16)

    def turn(w):
        tile = w_in.shape[2]

        def one(n, carry):
            at = pl.ds(pl.multiple_of(n * tile, tile), tile)
            t_in[w, :, at] = w_in[w, at, :].T
            t_out[w, at, :] = w_out[w, :, at].T
            return carry

        lax.fori_loop(0, 2 * half // tile, one, 0)

    def unpack(c, kind):
        all_here(c, kind)
        rows = rbuf[c, kind].astype(F32)
        flat = lambda part: part.reshape(n_dp * 8, 128)
        narrow = jnp.concatenate([flat(rows[:, 0:8]), flat(rows[:, 8:16])], axis=1)
        broad = jnp.where(path == 0, flat(rows[:, 16:24]), flat(rows[:, 24:32]))
        return narrow.astype(BF16), broad

    def prepare():
        for c in (0, 1):
            act, x = unpack(c, 0)
            act_rows[c] = act
            x_turned[c] = x.T.astype(BF16)

    def finish(c):
        grad_pre, grad_y = unpack(c, 1)
        gin_ref[0, c] = mm(x_turned[c], grad_pre)[:share]
        gout_ref[0, c] = mm(grad_y.T.astype(BF16), act_rows[c])[:share]

    early = 1 - chip // (chips // 2)

    def seeds():
        all_rows.wait()
        mine = lax.broadcasted_iota(jnp.int32, (16, 128), 0) + 8 * block
        every = lax.broadcasted_iota(jnp.int32, (128, 128), 0)

        def count(group, total):
            left, right = [], []
            for n in range(8):
                tile = ids_all[group * 8 + n]
                events = jnp.where(path == 0, tile[0:1, :], tile[1:2, :])
                left.append(jnp.where(mine == events, 1.0, 0.0).astype(BF16))
                right.append(jnp.where(every == tile[2:3, :], 1.0, 0.0).astype(BF16))
            return total + mm_t(jnp.concatenate(left, axis=1), jnp.concatenate(right, axis=1))

        counts = lax.fori_loop(0, n_dp // 8, count, jnp.zeros((16, 128), F32))[:8]
        sixteens = jnp.floor(counts * 0.0625)
        parts = jnp.concatenate([sixteens, counts - 16.0 * sixteens], axis=0).astype(BF16)
        sums = mm(parts, cand_ref[...])
        xs[2, 0] = fold((16.0 * sums[:8] + sums[8:]) * scale).astype(BF16)

    @pl.when(starts & (k == 0))
    def _():
        own_rows.wait()
        rows = first_rows[...].astype(F32)
        mine = jnp.where(block % 2 == 0, rows[:8], rows[8:])
        xs[0, 0] = fold(mine).astype(BF16)
        for copy in load(c1):
            copy.wait()
        add_branch(xs.at[0, 1], xs.at[0, 0], forward_one(0))

    @pl.when(relay)
    def _():
        for copy in load(c2):
            copy.start()

        @pl.when(k == 0)
        def _():
            all_rows.start()

    @pl.when(relay & (k > 0) & (k < last))
    def _():
        pl.semaphore_wait(barrier, 8)

    @pl.when(relay & edge)
    def _():
        pl.semaphore_wait(barrier, 7)

    @pl.when(jnp.logical_not(relay))
    def _():
        pl.semaphore_wait(barrier, 1)

    @pl.when(k == 0)
    def _():
        @pl.when(starts)
        def _():
            pass_on().start()

        @pl.when(jnp.logical_not(starts))
        def _():
            for copy in load(c1):
                copy.wait()
            pass_on().wait_recv()
            add_branch(
                give.at[0], xs.at[0, 1], forward_one(1), lambda j: hop(0, j, up).start()
            )

    @pl.when(jnp.logical_not(relay))
    def _():
        @pl.when(k == 0)
        def _():
            back().start()

        for copy in lend(c1):
            copy.start()
        for copy in lend(c1):
            copy.wait_send()
        for copy in lend(c2):
            copy.start()

        @pl.when(k > 0)
        def _():
            for copy in mail(0):
                copy.wait_recv()

        pl.semaphore_wait(met.at[5], 1)
        spread(0, 1 - own(0))
        for ph in (1, 2):
            for copy in mail(ph):
                copy.wait_recv()
            spread(ph, 1 - own(ph))
        prepare()

        @pl.when(k == 0)
        def _():
            finish(early)

        @pl.when(k > 0)
        def _():
            for copy in mail(3):
                copy.wait_recv()
            spread(3, 1 - own(3))
            finish(early)

        finish(1 - early)
        for copy in lend(c2):
            copy.wait_send()

        @pl.when(k == 0)
        def _():
            back().wait_send()

    @pl.when(relay)
    def _():
        def from_below(ph):
            def wait(j):
                @pl.when(k > 0)
                def _():
                    hop(ph, j, down).wait_recv()

            return wait

        def from_above(ph):
            def wait(j):
                @pl.when(k < last)
                def _():
                    hop(ph, j, up).wait_recv()

            return wait

        def to_above(ph):
            def send(j):
                @pl.when(k < last)
                def _():
                    hop(ph, j, up).start()

            return send

        def to_below(ph):
            def send(j):
                @pl.when(k > 0)
                def _():
                    hop(ph, j, down).start()

            return send

        def lent(blk):
            for copy in lend((c1, c2)[blk]):
                copy.wait_recv()

        def middle(ph):
            w = pairs[ph][0] if ph < 2 else pairs[3 - ph][1]
            weights = w_out if ph < 2 else t_in
            add_branch(xs.at[ph, 1], xs.at[ph, 0], [(twice(small[ph, 0]), weights, w)])

        def post(ph):
            for copy in mail(ph):
                copy.start()

        def settle(ph):
            middle(ph)
            post(ph)
            spread(ph, own(ph))

        def ready(blk):
            for copy in load((c1, c2)[blk]):
                copy.wait()

        def turn_and_meet():
            turn(c1)
            met_by(0)
            ready(1)
            turn(c2)
            met_by(1)

            @pl.when(k == 0)
            def _():
                lent(0)

            turn(2 + c1)
            met_by(2)
            lent(1)
            turn(2 + c2)
            met_by(3)

        @pl.when(k == 0)
        def _():
            meet(0, rounds[0])
            turn_and_meet()
            meet_other_plane()
            spread_ids()
            spread(0, own(0))
            between(0)
            between(1)
            many(ids_all.at[pl.ds(0, n_dp - 1)], ids_recv).wait()
            seeds()
            backward_sums(2, lambda j: None)
            back().wait_recv()

        @pl.when(k > 0)
        def _():
            meet(0, rounds[0])
            ready(0)
            lent(0)
            between(0)

            @pl.when(k > 1)
            def _():
                met_by(0)

            @pl.when(k == last)
            def _():
                met_by(1)
                met_by(2)
                met_by(3)
                ready(1)
                lent(1)
                between(1)

            forward_pair(0, from_below(0), to_above(0))

            @pl.when(k == last)
            def _():
                xs[1, 0] = give[0]

            @pl.when(k == 1)
            def _():
                turn_and_meet()
                between(1)
                meet_other_plane()
                settle(0)

            @pl.when((k > 1) & (k < last))
            def _():
                met_by(1)
                met_by(2)
                met_by(3)
                ready(1)
                lent(1)
                between(1)

        forward_pair(1, from_above(1), to_below(1))

        @pl.when(k > 0)
        def _():
            @pl.when(k > 1)
            def _():
                meet_other_plane()

                @pl.when(k == last)
                def _():
                    spread_ids()

            settle(1)

            @pl.when(k > 1)
            def _():
                settle(0)
                for w in range(4):
                    turn(w)

        @pl.when(k > 0)
        def _():
            backward_sums(2, lambda j: hop(2, j, down).wait_recv())

        parts = backward_pair(2)
        add_branch(give.at[2], xs.at[2, 0], parts, to_above(2))

        @pl.when(k < last)
        def _():
            @pl.when(k == 0)
            def _():
                settle(1)

            settle(2)
            prepare()

            @pl.when(k == 0)
            def _():
                finish(early)

        @pl.when(k == last)
        def _():
            xs[3, 0] = give[2]

        backward_sums(3, from_above(3))
        parts = backward_pair(3)

        @pl.when(k > 0)
        def _():
            add_branch(give.at[3], xs.at[3, 0], parts, to_below(3))
            settle(3)

        @pl.when(k == 0)
        def _():
            @pl.when(path == 0)
            def _():
                spread(3, 0)
                middle(3)
                spread(3, 1, True)

            @pl.when(path == 1)
            def _():
                spread(3, 0, True)
                middle(3)
                spread(3, 1)

        @pl.when(k == last)
        def _():
            settle(2)
            prepare()

        @pl.when(k > 0)
        def _():
            finish(early)

        finish(1 - early)

        @pl.when(k < last)
        def _():
            for j in pieces:
                hop(2, j, up).wait_send()

        @pl.when((k > 0) & (k < last))
        def _():
            for j in pieces:
                hop(0, j, up).wait_send()

        @pl.when(k > 0)
        def _():
            for j in pieces:
                hop(1, j, down).wait_send()
                hop(3, j, down).wait_send()
            for ph in (0, 3):
                for copy in mail(ph):
                    copy.wait_send()

        for ph in (1, 2):
            for copy in mail(ph):
                copy.wait_send()

        @pl.when(k == 0)
        def _():
            many(rbuf.at[0, 0], x_send.at[2, 1]).wait()

        @pl.when(k == last)
        def _():
            many(ids_all.at[pl.ds(0, n_dp - 1)], ids_recv).wait()

        @pl.when(edge)
        def _():
            many(ids_all.at[pl.ds(0, n_dp - 1)], ids_send).wait()

    @pl.when(k == 0)
    def _():
        @pl.when(starts)
        def _():
            pass_on().wait_send()

        @pl.when(jnp.logical_not(starts))
        def _():
            for j in pieces:
                hop(0, j, up).wait_send()

    def gone(c, kind):
        many(rbuf.at[c, kind, pl.ds(0, n_dp - 1)], x_send.at[c, kind]).wait()

    for ph in range(3):
        gone(cs[ph], ph // 2)

    @pl.when(jnp.logical_not(spared))
    def _():
        gone(cs[3], 1)


def local(n_pipe, n_dp, item_ids, plan_order, candidates, adapters_in, adapters_out):
    batches, width = item_ids.shape
    events = width - 1
    _, _, features, hidden = adapters_in.shape
    share = features // n_dp
    scale = 1.0 / math.sqrt(batches * n_dp * events)
    spare = width - plan_order.shape[0]
    ids = lax.pad(item_ids, 0, ((0, 1, 0), (0, 0, 0))) + lax.pad(
        plan_order[None, :], 0, ((batches, 0, 0), (0, spare, 0))
    )
    vmem = pl.BlockSpec(memory_space=pltpu.VMEM)
    hbm = pl.BlockSpec(memory_space=pltpu.HBM)
    grad_in, grad_out = pl.pallas_call(
        functools.partial(kernel, n_pipe, n_dp, scale),
        out_shape=(
            jax.ShapeDtypeStruct((1, 2, share, hidden), F32),
            jax.ShapeDtypeStruct((1, 2, share, hidden), F32),
        ),
        in_specs=[hbm] * 4,
        out_specs=(vmem, vmem),
        scratch_shapes=[
            pltpu.VMEM((4, features, hidden), BF16),
            pltpu.VMEM((4, hidden, features), BF16),
            pltpu.VMEM((4, hidden, features), BF16),
            pltpu.VMEM((4, features, hidden), BF16),
            pltpu.VMEM((2, hidden, hidden), BF16),
            pltpu.VMEM((2, hidden, hidden), BF16),
            pltpu.VMEM(ids.shape, jnp.int32),
            pltpu.VMEM(candidates.shape, BF16),
            pltpu.VMEM((16, features), BF16),
            pltpu.VMEM((8, 128), jnp.int32),
            pltpu.VMEM((n_dp, 8, 128), jnp.int32),
            pltpu.VMEM((4, 2, 16, features // 2), BF16),
            pltpu.VMEM((4, 16, features // 2), BF16),
            pltpu.VMEM((4, 2, 8, hidden), F32),
            pltpu.VMEM((4, 8, hidden), F32),
            pltpu.VMEM((2, 8, hidden), F32),
            pltpu.VMEM((3, 2, n_dp // 2, 32, 128), BF16),
            pltpu.VMEM((2, 2, n_dp, 32, 128), BF16),
            pltpu.VMEM((2, 128, n_dp * 8), BF16),
            pltpu.VMEM((2, n_dp * 8, hidden), BF16),
            pltpu.SemaphoreType.DMA((2, 2)),
            pltpu.SemaphoreType.DMA((3,)),
            pltpu.SemaphoreType.DMA((2, 2)),
            pltpu.SemaphoreType.DMA((2, 2)),
            pltpu.SemaphoreType.DMA((4, PIECES)),
            pltpu.SemaphoreType.DMA((4, PIECES)),
            pltpu.SemaphoreType.DMA((4, 2)),
            pltpu.SemaphoreType.DMA((4, 2)),
            pltpu.SemaphoreType.DMA,
            pltpu.SemaphoreType.DMA,
            pltpu.SemaphoreType.DMA,
            pltpu.SemaphoreType.DMA,
            pltpu.SemaphoreType.DMA,
            pltpu.SemaphoreType.DMA,
            pltpu.SemaphoreType.DMA((3, 2)),
            pltpu.SemaphoreType.DMA((2, 2)),
            pltpu.SemaphoreType.REGULAR((6,)),
        ],
        compiler_params=pltpu.CompilerParams(
            collective_id=0, has_side_effects=True, vmem_limit_bytes=107 * 512 * 1024
        ),
    )(ids, candidates, adapters_in, adapters_out)
    return grad_in, jnp.swapaxes(grad_out, 2, 3)


def solution(mesh):
    in_specs = (P(None, "dp"), P(), P(), P("pipe", None, None, None), P("pipe", None, None, None))
    out_specs = (P("pipe", None, "dp", None), P("pipe", None, None, "dp"))
    return jax.shard_map(
        functools.partial(local, mesh.shape["pipe"], mesh.shape["dp"]),
        mesh=mesh,
        in_specs=in_specs,
        out_specs=out_specs,
        check_vma=False,
    )
```
